512 devices in a mesh: ia: 4 (over x), ja: 16 (over z, core), ka: 8 (over y).
Axes of the slice: x: 4, y: 8, z: 8, core: 2. Of those that a mesh axis runs over, the one named last changes fastest.
Arguments:
- tensor: bfloat16 [512, 512, 1024], P('ia', 'ja', 'ka'), may hold values from -21000 to 21000
- factor_b: float32 [16, 32, 32], P('ja', ('ia', 'ka')), may hold values from -6 to 6
- factor_c: float32 [8, 128, 32], P('ka', ('ia', 'ja')), may hold values from -6 to 6
Outputs:
- factor_a_out: float32 [4, 128, 32], P('ia', ('ja', 'ka'))
- factor_b_out: float32 [16, 32, 32], P('ja', ('ia', 'ka'))
- factor_c_out: float32 [8, 128, 32], P('ka', ('ia', 'ja'))
The draws below stay inside these ranges and needn't reach their ends.
All inputs are finite; a program needn't handle non-finite values.
Results may differ from the reference program's by a relative error of at most 0.0041.
Values may be sent and summed in bfloat16 or wider, within the bound.
No kernel may reach another device: no remote copies, remote signals or barrier semaphores. Data moves between devices by JAX's collectives and lax.ppermute only.
A program may use at most 64 MiB of HBM per device.

```python
import math
import jax
import jax.numpy as jnp
from jax import lax

BI = 128
BJ = 32
BK = 128
R = 32
SWEEPS = 1
BLOCKS_I = 4
BLOCKS_J = 16
BLOCKS_K = 8
I = 512
J = 512
K = 1024


def mode_scales(key, length, top):
    ramp = jnp.arange(length).astype(jnp.float32) / length
    rough = jnp.exp(jax.random.uniform(key, (length,), jnp.float32, -0.35, 0.35))
    return top ** ramp * rough


def draw_tensor(key, part):
    key = jax.random.fold_in(key, 11)
    keys = jax.random.split(key, 4)
    values = jnp.clip(jax.random.normal(keys[0], (I, J, K), jnp.float32), -4.0, 4.0)
    top = 10.0
    first = mode_scales(keys[1], I, top)
    second = mode_scales(keys[2], J, top)
    third = mode_scales(keys[3], K, top)
    scaled = values * first[:, None, None] * second[None, :, None] * third[None, None, :]
    return scaled.astype(jnp.bfloat16)


def block_scale(stream_key, dims, shards, low, largest):
    loudness, own = 1.0, jax.random.fold_in(stream_key, 6)
    for dim, parts in shards:
        draws = jnp.exp(jax.random.uniform(jax.random.fold_in(own, dim), (parts,), jnp.float32, low / len(shards), largest / len(shards)))
        loudness = loudness * jnp.repeat(draws, dims[dim] // parts).reshape([-1 if axis == dim else 1 for axis in range(len(dims))])
    return loudness


def normal_values(rng, shape, deviation, limit, cuts=(), held_as=jnp.bfloat16):
    result = deviation * jax.random.normal(rng, shape, jnp.float32)
    if cuts:
        result = result * block_scale(rng, shape, cuts, -0.22, 0.18)
    return jnp.clip(result, -limit, limit).astype(held_as)


def setup_inputs(seed: int = 0) -> dict:
    splits = jax.random.split(jax.random.key(seed), 4)
    tensor = draw_tensor(jax.random.fold_in(splits[3], 71), 0)
    factor_b = normal_values(splits[1], (BLOCKS_J, BJ, R), 1.0, 6.0, ((0, 16), (1, 32)), jnp.float32)
    factor_c = normal_values(splits[2], (BLOCKS_K, BK, R), 1.0, 6.0, ((0, 8), (1, 64)), jnp.float32)
    return {"tensor": tensor, "factor_b": factor_b, "factor_c": factor_c}


HIGH = lax.Precision.HIGHEST

def gram_of(matrix):
    return jnp.dot(matrix.T, matrix, precision=HIGH)

def solve_rows(summed, vmatrix):
    lower_factor = jnp.linalg.cholesky(vmatrix)
    forward = lax.linalg.triangular_solve(lower_factor, summed.T, left_side=True, lower=True)
    backward = lax.linalg.triangular_solve(lower_factor, forward, left_side=True, lower=True, transpose_a=True)
    return backward.T

def rescale(solved, gram_raw, total):
    factor_scale = lax.rsqrt(jnp.diagonal(gram_raw) / total + 1e-06)
    return (solved * factor_scale[None, :], gram_raw * factor_scale[:, None] * factor_scale[None, :])

def update(summed, vmatrix, total):
    solved = solve_rows(summed, vmatrix)
    return rescale(solved, gram_of(solved), total)

def contract_last(tensor, c_low):
    block_rows = math.gcd(I, 64)
    block_count = I // block_rows
    pieces = tensor.reshape(block_count, block_rows, J, K)
    c_wide = c_low.astype(jnp.float32)

    def over_block(tensor_piece):
        return jnp.einsum('ijk,kr->rij', tensor_piece.astype(jnp.float32), c_wide, precision=HIGH)
    results = lax.map(over_block, pieces)
    return jnp.transpose(results, (1, 0, 2, 3)).reshape(R, I, J)

def contract_first(tensor, a_low):
    block_rows = math.gcd(I, 64)
    block_count = I // block_rows
    pieces = tensor.reshape(block_count, block_rows, J, K)
    a_pieces = a_low.astype(jnp.float32).reshape(block_count, block_rows, R)

    def add_block(running, paired):
        tensor_piece, a_piece = paired
        return (running + jnp.einsum('ijk,ir->rjk', tensor_piece.astype(jnp.float32), a_piece, precision=HIGH), None)
    start_total = jnp.zeros((R, J, K), jnp.float32)
    running, unused = lax.scan(add_block, start_total, (pieces, a_pieces))
    return running

def reference(tensor, factor_b, factor_c):
    mode_b = factor_b.reshape(J, R)
    mode_c = factor_c.reshape(K, R)
    gram_b = gram_of(mode_b)
    gram_c = gram_of(mode_c)
    mode_a = jnp.zeros((I, R), jnp.float32)
    for sweep_index in range(SWEEPS):
        along_k = contract_last(tensor, mode_c.astype(jnp.bfloat16))
        summed_a = jnp.einsum('rij,jr->ir', along_k, mode_b, precision=HIGH)
        mode_a, gram_a = update(summed_a, gram_b * gram_c, I)
        summed_b = jnp.einsum('rij,ir->jr', along_k, mode_a, precision=HIGH)
        mode_b, gram_b = update(summed_b, gram_a * gram_c, J)
        along_i = contract_first(tensor, mode_a.astype(jnp.bfloat16))
        summed_c = jnp.einsum('rjk,jr->kr', along_i, mode_b, precision=HIGH)
        mode_c, gram_c = update(summed_c, gram_a * gram_b, K)
    return (mode_a.reshape(BLOCKS_I, BI, R), mode_b.reshape(BLOCKS_J, BJ, R), mode_c.reshape(BLOCKS_K, BK, R))
```

```python
import jax
import jax.numpy as jnp
from jax import lax
from jax.experimental import pallas as pl
from jax.experimental.pallas import tpu as pltpu
from jax.sharding import PartitionSpec as P

HIGH = lax.Precision.HIGHEST
F32 = jnp.float32
BF16 = jnp.bfloat16
R = 32
LANES = 128
PACK = LANES // R


def dot(left, right, dims=((1,), (0,))):
    return lax.dot_general(
        left, right, (dims, ((), ())), precision=HIGH, preferred_element_type=F32
    )


def pack(matrix):
    rows = matrix.shape[0] // PACK
    return jnp.concatenate([matrix[g * rows : (g + 1) * rows] for g in range(PACK)], axis=1)


def unpack(packed):
    return jnp.concatenate([packed[:, g * R : (g + 1) * R] for g in range(PACK)], axis=0)


def eye():
    rows = lax.broadcasted_iota(jnp.int32, (R, R), 0)
    cols = lax.broadcasted_iota(jnp.int32, (R, R), 1)
    return (rows == cols).astype(F32)


def inverse(matrix):
    work = jnp.concatenate([matrix, eye()], axis=1)
    rows = lax.broadcasted_iota(jnp.int32, (R, 1), 0)
    for p in range(R):
        pivot_row = work[p : p + 1, :] / work[p : p + 1, p : p + 1]
        column = work[:, p : p + 1] - (rows == p).astype(F32)
        work = work - column * pivot_row
    return work[:, R : 2 * R]


def scales(gram_raw, total):
    diagonal = gram_raw * eye()
    row = lax.rsqrt(jnp.sum(diagonal, axis=0, keepdims=True) / total + 1e-06)
    column = lax.rsqrt(jnp.sum(diagonal, axis=1, keepdims=True) / total + 1e-06)
    return row, column


def call(kernel, outs, args, flops, scalars=0):
    spec = [pl.BlockSpec(memory_space=pltpu.SMEM)] * scalars
    spec += [pl.BlockSpec(memory_space=pltpu.VMEM)] * (len(args) - scalars)
    moved = sum(4 * a.size for a in args) + sum(4 * o.size for o in outs)
    return pl.pallas_call(
        kernel,
        out_shape=outs,
        in_specs=spec,
        out_specs=[pl.BlockSpec(memory_space=pltpu.VMEM)] * len(outs),
        compiler_params=pltpu.CompilerParams(vmem_limit_bytes=24 * 2**20),
        cost_estimate=pl.CostEstimate(flops=flops, bytes_accessed=moved, transcendentals=0),
    )(*args)


def shape(*dims, dtype=F32):
    return jax.ShapeDtypeStruct(dims, dtype)


def weights_kernel(all_ref, weights_ref, gram_ref):
    rows = all_ref[...]
    products = dot(rows, rows, ((0,), (0,)))
    gram_b = products[0:R, 0:R]
    gram_c = products[R : 2 * R, R : 2 * R] + products[2 * R : 3 * R, 2 * R : 3 * R]
    gram_ref[...] = gram_c
    weights_ref[...] = inverse(gram_b * gram_c)


def first_kernel(sizes, place_ref, all_ref, tensor_ref, send_ref, along_ref):
    n_ia, n_ja, n_ka = sizes
    rows_i, rows_j, rows_k = tensor_ref.shape
    ja, ka = place_ref[1], place_ref[2]
    devices = n_ia * n_ja * n_ka
    k_of = lax.broadcasted_iota(jnp.int32, (rows_k, devices), 0)
    d_of = lax.broadcasted_iota(jnp.int32, (rows_k, devices), 1)
    own = d_of == (k_of >> 1) * n_ka + ka
    odd = (k_of & 1) == 1
    low = all_ref[...].astype(BF16)
    even_rows = jnp.where(own & ~odd, 1.0, 0.0).astype(BF16)
    odd_rows = jnp.where(own & odd, 1.0, 0.0).astype(BF16)
    block_c = jnp.dot(even_rows, low[:, R : 2 * R], preferred_element_type=F32)
    block_c += jnp.dot(odd_rows, low[:, 2 * R : 3 * R], preferred_element_type=F32)
    block_b = jnp.concatenate(
        [
            all_ref[pl.ds(pl.multiple_of((ia * n_ja + ja) * n_ka, n_ka), n_ka), 0:R]
            for ia in range(n_ia)
        ],
        axis=0,
    )
    flat = tensor_ref[...].reshape(rows_i * rows_j, rows_k)
    along = jnp.dot(flat, block_c.astype(BF16), preferred_element_type=F32)
    along_ref[...] = along
    terms = along.reshape(rows_i, rows_j, R) * block_b[None]
    packed = pack(jnp.sum(terms, axis=1))
    half = packed.shape[0] // 2
    peers = send_ref.shape[0] // 2
    send_ref[0:peers] = jnp.broadcast_to(packed[None, :half], (peers, half, LANES))
    send_ref[peers:] = jnp.broadcast_to(packed[None, half:], (peers, half, LANES))


def sum_kernel(got_ref, send_ref):
    total = jnp.sum(got_ref[...], axis=0)
    send_ref[...] = jnp.broadcast_to(total[None], send_ref.shape)


def halves(got):
    pairs = got.shape[0] // 2
    first = got[0]
    second = got[1]
    for n in range(1, pairs):
        first += got[2 * n]
        second += got[2 * n + 1]
    return jnp.concatenate([first, second], axis=0)


def second_kernel(got_ref, weights_ref, along_ref, send_ref, solved_ref):
    summed = unpack(halves(got_ref[...]))
    solved = dot(summed, weights_ref[...])
    solved_ref[...] = solved
    rows_i = solved.shape[0]
    rows_j = along_ref.shape[0] // rows_i
    gram = dot(solved, solved, ((0,), (0,)))
    terms = along_ref[...].reshape(rows_i, rows_j, R) * solved[:, None, :]
    part = jnp.concatenate([pack(jnp.sum(terms, axis=0)), pack(gram)], axis=0)
    send_ref[...] = jnp.broadcast_to(part[None], send_ref.shape)


def third_kernel(
    totals, copies, got_ref, solved_ref, gram_c_ref, turned_ref,
    send_ref, gram_a_ref, gram_b_ref, factor_a_ref, solved_b_ref,
):
    total = jnp.sum(got_ref[...], axis=0)
    half = total.shape[0] // 2
    gram_raw = unpack(total[half:]) * (1.0 / copies)
    row, column = scales(gram_raw, totals[0])
    gram_a = gram_raw * row * column
    gram_a_ref[...] = gram_a
    factor_a = solved_ref[...] * row
    factor_a_ref[...] = factor_a
    summed = unpack(total[:half]) * row
    solved_b = dot(summed, inverse(gram_a * gram_c_ref[...]))
    solved_b_ref[...] = solved_b
    gram_b_ref[...] = pack(dot(solved_b, solved_b, ((0,), (0,))))
    a_low = factor_a.astype(BF16).T
    b_turned = solved_b.T
    part = jnp.zeros((R, turned_ref.shape[2]), F32)
    for j in range(turned_ref.shape[0]):
        along = jnp.dot(a_low, turned_ref[j], preferred_element_type=F32)
        part += along * b_turned[:, j : j + 1]
    half = R // 2
    peers = send_ref.shape[0] // 2
    for n in range(peers):
        send_ref[2 * n] = part[:half]
        send_ref[2 * n + 1] = part[half:]


def pass_kernel(got_ref, gram_ref, send_ref):
    total = jnp.concatenate([jnp.sum(got_ref[...], axis=0), gram_ref[...]], axis=0)
    send_ref[...] = jnp.broadcast_to(total[None], send_ref.shape)


def fourth_kernel(
    totals, sizes, place_ref, got_ref, gram_a_ref, factor_a_ref, solved_b_ref,
    send_ref, out_a_ref, out_b_ref, own_c_ref,
):
    n_ia, n_ja, n_ka = sizes
    ia, ja, ka = place_ref[0], place_ref[1], place_ref[2]
    half = R // 2
    summed = halves(got_ref[:, 0:half, :])
    gram_raw = unpack(jnp.sum(got_ref[:, half:, :], axis=0))
    row, column = scales(gram_raw, totals[1])
    gram_b = gram_raw * row * column
    out_a_ref[...] = factor_a_ref[pl.ds(ja * n_ka + ka, 1), :]
    out_b_ref[...] = solved_b_ref[pl.ds(ia * n_ka + ka, 1), :] * row
    solved = dot(inverse(gram_a_ref[...] * gram_b), summed * column)
    squares = dot(jnp.ones((8, solved.shape[1]), F32), solved * solved, ((1,), (1,)))
    squares = jnp.concatenate([squares, jnp.zeros((8, LANES - R), F32)], axis=1)
    send_ref[...] = jnp.broadcast_to(squares[None], send_ref.shape)
    k_of = lax.broadcasted_iota(jnp.int32, (8, solved.shape[1]), 1)
    t_of = lax.broadcasted_iota(jnp.int32, (8, solved.shape[1]), 0)
    chosen = jnp.where(k_of == 2 * (ia * n_ja + ja) + t_of, 1.0, 0.0)
    own_c_ref[...] = dot(chosen, solved, ((1,), (1,)))


def last_kernel(total, got_ref, own_c_ref, out_ref):
    squares = jnp.sum(got_ref[...], axis=0)[0:1, 0:R]
    out_ref[...] = own_c_ref[0:2, :] * lax.rsqrt(squares / total + 1e-06)


def exchange(blocks, axes, groups=None):
    return lax.all_to_all(blocks, axes, 0, 0, tiled=True, axis_index_groups=groups)


def local(tensor, factor_b, factor_c):
    rows_i, rows_j, rows_k = tensor.shape
    sizes = tuple(lax.axis_size(axis) for axis in ("ia", "ja", "ka"))
    n_ia, n_ja, n_ka = sizes
    totals = (rows_i * n_ia, rows_j * n_ja, rows_k * n_ka)
    devices = n_ia * n_ja * n_ka
    cores = 2
    place = jnp.stack([lax.axis_index(axis) for axis in ("ia", "ja", "ka")]).astype(jnp.int32)
    plane = [
        [(z * cores + core) * n_ka + y for core in range(cores) for y in range(n_ka)]
        for z in range(n_ja // cores)
    ]
    line = [
        [x * n_ja + z * cores + core for x in range(n_ia) for core in range(cores)]
        for z in range(n_ja // cores)
    ]
    own = jnp.concatenate(
        [factor_b.reshape(1, R), factor_c.reshape(1, 2 * R), jnp.zeros((1, R), F32)], axis=1
    )
    rows = exchange(jnp.broadcast_to(own, (devices, LANES)), ("ia", "ja", "ka"))
    turned = jnp.transpose(tensor, (1, 0, 2))
    weights_a, gram_c = call(
        weights_kernel, [shape(R, R), shape(R, R)], [rows], 2**24
    )
    send, along = call(
        lambda *refs: first_kernel(sizes, *refs),
        [shape(cores * n_ka, R // 2, LANES), shape(rows_i * rows_j, R)],
        [place, rows, tensor],
        2**26,
        scalars=1,
    )
    got = exchange(send, ("ja", "ka"), plane)
    (send,) = call(sum_kernel, [shape(n_ja, R // 2, LANES)], [got], 2**16)
    got = exchange(send, "ja")
    send, solved_a = call(
        second_kernel, [shape(n_ia * n_ka, 16, LANES), shape(rows_i, R)], [got, weights_a, along], 2**24
    )
    got = exchange(send, ("ia", "ka"))
    send, gram_a, gram_b, factor_a, solved_b = call(
        lambda *refs: third_kernel(totals, n_ka, *refs),
        [
            shape(n_ia * cores, R // 2, LANES),
            shape(R, R),
            shape(R // PACK, LANES),
            shape(rows_i, R),
            shape(rows_j, R),
        ],
        [got, solved_a, gram_c, turned],
        2**26,
    )
    got = exchange(send, ("ia", "ja"), line)
    (send,) = call(pass_kernel, [shape(n_ja, 24, LANES)], [got, gram_b], 2**16)
    got = exchange(send, "ja")
    send, out_a, out_b, own_c = call(
        lambda *refs: fourth_kernel(totals, sizes, *refs),
        [shape(n_ka, 8, LANES), shape(1, R), shape(1, R), shape(8, R)],
        [place, got, gram_a, factor_a, solved_b],
        2**22,
        scalars=1,
    )
    got = exchange(send, "ka")
    (out_c,) = call(
        lambda *refs: last_kernel(totals[2], *refs), [shape(2, R)], [got, own_c], 2**12
    )
    return out_a[None], out_b[None], out_c[None]


def solution(mesh):
    placed = (P("ia", "ja", "ka"), P("ja", ("ia", "ka"), None), P("ka", ("ia", "ja"), None))
    return jax.shard_map(
        local,
        mesh=mesh,
        in_specs=placed,
        out_specs=(
            P("ia", ("ja", "ka"), None),
            P("ja", ("ia", "ka"), None),
            P("ka", ("ia", "ja"), None),
        ),
        check_vma=False,
    )
```

```python
import jax
import jax.numpy as jnp
from jax import lax
from jax.experimental import pallas as pl
from jax.experimental.pallas import tpu as pltpu
from jax.sharding import PartitionSpec as P

HIGH = lax.Precision.HIGHEST
F32 = jnp.float32
BF16 = jnp.bfloat16
R = 32
LANES = 128
PACK = LANES // R
SUB = R // PACK


def dot(left, right, dims=((1,), (0,))):
    return lax.dot_general(
        left, right, (dims, ((), ())), precision=HIGH, preferred_element_type=F32
    )


def pack(matrix):
    rows = matrix.shape[0] // PACK
    return jnp.concatenate([matrix[g * rows : (g + 1) * rows] for g in range(PACK)], axis=1)


def unpack(packed):
    return jnp.concatenate([packed[:, g * R : (g + 1) * R] for g in range(PACK)], axis=0)


def lane_groups(matrix):
    total = matrix[0:R, 0:R]
    for g in range(1, PACK):
        total += matrix[g * R : (g + 1) * R, g * R : (g + 1) * R]
    return total


def eye():
    rows = lax.broadcasted_iota(jnp.int32, (R, R), 0)
    cols = lax.broadcasted_iota(jnp.int32, (R, R), 1)
    return (rows == cols).astype(F32)


def inverse(packed):
    work = packed
    lane = lax.broadcasted_iota(jnp.int32, (SUB, LANES), 1)
    sub = lax.broadcasted_iota(jnp.int32, (SUB, LANES), 0)
    group, place = lane // R, lane % R
    for p in range(PACK):
        in_rows = group == p
        in_cols = place // SUB == p
        spread = [jnp.broadcast_to(work[s : s + 1, :], (SUB, LANES)) for s in range(SUB)]
        cols = [
            jnp.where(
                in_rows,
                jnp.where(sub == s, -1.0, 0.0),
                jnp.take_along_axis(work, group * R + p * SUB + s, axis=1),
            )
            for s in range(SUB)
        ]
        rows = [
            jnp.where(
                in_cols,
                jnp.where(place == p * SUB + s, 1.0, 0.0),
                jnp.take_along_axis(spread[s], p * R + place, axis=1),
            )
            for s in range(SUB)
        ]
        pivots = [[None] * SUB for _ in range(SUB)]
        for s in range(SUB):
            for t in range(s, SUB):
                where = jnp.full((SUB, LANES), p * R + p * SUB + t, jnp.int32)
                pivots[s][t] = pivots[t][s] = jnp.take_along_axis(spread[s], where, axis=1)
        for t in range(SUB):
            recip = 1.0 / pivots[t][t]
            rows[t] = rows[t] * recip
            for u in range(t + 1, SUB):
                pivots[t][u] = pivots[t][u] * recip
            for s in range(SUB):
                if s != t:
                    factor = pivots[s][t]
                    rows[s] = rows[s] - factor * rows[t]
                    for u in range(t + 1, SUB):
                        pivots[s][u] = pivots[s][u] - factor * pivots[t][u]
        work = jnp.where(in_rows | in_cols, 0.0, work)
        for col, row in zip(cols, rows):
            work = work - col * row
    return work


def scales(gram_raw, total):
    diagonal = gram_raw * eye()
    row = lax.rsqrt(jnp.sum(diagonal, axis=0, keepdims=True) / total + 1e-06)
    column = lax.rsqrt(jnp.sum(diagonal, axis=1, keepdims=True) / total + 1e-06)
    return row, column


def call(kernel, outs, args, flops, scalars=0):
    spec = [pl.BlockSpec(memory_space=pltpu.SMEM)] * scalars
    spec += [pl.BlockSpec(memory_space=pltpu.VMEM)] * (len(args) - scalars)
    moved = sum(4 * a.size for a in args) + sum(4 * o.size for o in outs)
    return pl.pallas_call(
        kernel,
        out_shape=outs,
        in_specs=spec,
        out_specs=[pl.BlockSpec(memory_space=pltpu.VMEM)] * len(outs),
        compiler_params=pltpu.CompilerParams(vmem_limit_bytes=24 * 2**20),
        cost_estimate=pl.CostEstimate(flops=flops, bytes_accessed=moved, transcendentals=0),
    )(*args)


def shape(*dims, dtype=F32):
    return jax.ShapeDtypeStruct(dims, dtype)


def own_kernel(b_ref, c_ref, send_ref):
    row = jnp.concatenate(
        [b_ref[...], c_ref[0:1, :], c_ref[1:2, :], jnp.zeros((1, LANES - 3 * R), F32)], axis=1
    )
    send_ref[...] = jnp.broadcast_to(row, send_ref.shape)


def along_kernel(sizes, place_ref, rows_ref, tensor_ref, send_ref):
    n_ia, n_ja, n_ka = sizes
    rows_i, rows_j, rows_k = tensor_ref.shape
    ja = place_ref[1]
    rows = rows_ref[...]
    sources = rows.shape[0]
    k_of = lax.broadcasted_iota(jnp.int32, (rows_k, sources), 0)
    d_of = lax.broadcasted_iota(jnp.int32, (rows_k, sources), 1)
    low = rows.astype(BF16)
    even = jnp.where(k_of == 2 * d_of, 1.0, 0.0).astype(BF16)
    odd = jnp.where(k_of == 2 * d_of + 1, 1.0, 0.0).astype(BF16)
    block_c = jnp.dot(even, low[:, R : 2 * R], preferred_element_type=F32)
    block_c += jnp.dot(odd, low[:, 2 * R : 3 * R], preferred_element_type=F32)
    tiled = jnp.concatenate([block_c] * PACK, axis=1)
    lane = lax.broadcasted_iota(jnp.int32, (rows_k, LANES), 1) // R
    weights = jnp.concatenate(
        [jnp.where(lane == g, tiled, 0.0).astype(BF16) for g in range(PACK)], axis=0
    )
    low_i = rows_i // (PACK * n_ka)
    sums = low_i * rows_j
    for ka in range(n_ka):
        left = jnp.concatenate(
            [
                tensor_ref[(g * n_ka + ka) * low_i : (g * n_ka + ka + 1) * low_i].reshape(sums, rows_k)
                for g in range(PACK)
            ],
            axis=1,
        )
        send_ref[ka, 0:sums, :] = jnp.dot(left, weights, preferred_element_type=F32)
    products = dot(rows, rows, ((0,), (0,)))
    gram_b = products[0:R, 0:R]
    gram_c = products[R : 2 * R, R : 2 * R] + products[2 * R : 3 * R, 2 * R : 3 * R]
    own_b = jnp.concatenate(
        [rows_ref[pl.ds(ia * n_ja + ja, 1), 0:R] for ia in range(n_ia)], axis=1
    )
    upper = lax.broadcasted_iota(jnp.int32, (R, R), 0) <= lax.broadcasted_iota(jnp.int32, (R, R), 1)
    diagonal = jnp.sum(gram_c * eye(), axis=0, keepdims=True)
    riders = jnp.concatenate(
        [
            pack(jnp.where(upper, gram_b, gram_c)),
            own_b,
            jnp.concatenate([diagonal, jnp.zeros((1, LANES - R), F32)], axis=1),
            jnp.zeros((SUB - 2, LANES), F32),
        ],
        axis=0,
    )
    for ka in range(n_ka):
        send_ref[ka, sums:, :] = riders


def first_kernel(low_i, got_ref, send_ref, along_ref, grams_ref):
    sums = got_ref.shape[1] - 2 * SUB
    along = jnp.sum(got_ref[:, 0:sums, :], axis=0)
    along_ref[...] = along
    grams_ref[...] = jnp.sum(got_ref[:, sums:, :], axis=0)
    own_b = jnp.concatenate(
        [got_ref[ka, sums + SUB : sums + SUB + 1, :] for ka in range(got_ref.shape[0])], axis=0
    )
    block_b = unpack(own_b)
    rows_j = block_b.shape[0]
    wide_b = jnp.concatenate([block_b] * PACK, axis=1)
    terms = along.reshape(low_i, rows_j, LANES) * wide_b[None]
    summed = jnp.concatenate(
        [jnp.sum(terms, axis=1), jnp.zeros((8 - low_i, LANES), F32)], axis=0
    )
    send_ref[...] = jnp.broadcast_to(summed[None], send_ref.shape)


def weights_kernel(grams_ref, weights_ref, gram_ref):
    mixed = unpack(grams_ref[0:SUB])
    turned = mixed.T
    rows = lax.broadcasted_iota(jnp.int32, (R, R), 0)
    cols = lax.broadcasted_iota(jnp.int32, (R, R), 1)
    gram_b = jnp.where(rows <= cols, mixed, turned)
    gram_c = jnp.where(rows > cols, mixed, jnp.where(rows == cols, grams_ref[SUB + 1 : SUB + 2, 0:R], turned))
    gram_ref[...] = gram_c
    one = unpack(inverse(pack(gram_b * gram_c)))
    tiled = jnp.concatenate([jnp.concatenate([one] * PACK, axis=1)] * PACK, axis=0)
    rows = lax.broadcasted_iota(jnp.int32, (LANES, LANES), 0) // R
    cols = lax.broadcasted_iota(jnp.int32, (LANES, LANES), 1) // R
    weights_ref[...] = jnp.where(rows == cols, tiled, 0.0)


def second_kernel(low_i, got_ref, weights_ref, along_ref, send_ref):
    summed = jnp.sum(got_ref[...], axis=0)
    solved = dot(summed, weights_ref[...])[0:low_i]
    rows_j = along_ref.shape[0] // low_i
    terms = along_ref[...].reshape(low_i, rows_j, LANES) * solved[:, None, :]
    wide = jnp.sum(terms, axis=0)
    part = wide[:, 0:R]
    for g in range(1, PACK):
        part += wide[:, g * R : (g + 1) * R]
    rows = jnp.concatenate([pack(part), solved], axis=0)
    send_ref[...] = jnp.broadcast_to(rows[None], send_ref.shape)


def third_kernel(
    totals, sizes, place_ref, got_ref, gram_c_ref, turned_ref,
    send_ref, gram_a_ref, factor_a_ref, solved_b_ref,
):
    n_ia, n_ja, n_ka = sizes
    ia = place_ref[0]
    peers, _, _ = got_ref.shape
    low_i = got_ref.shape[1] - SUB
    total = jnp.sum(got_ref[:, 0:SUB, :], axis=0)
    everyone = jnp.concatenate([got_ref[n, SUB:, :] for n in range(peers)], axis=0)
    gram_raw = lane_groups(dot(everyone, everyone, ((0,), (0,))))
    row, column = scales(gram_raw, totals[0])
    gram_a = gram_raw * row * column
    gram_a_ref[...] = gram_a
    solved_a = unpack(
        jnp.concatenate([got_ref[ia * n_ka + ka, SUB:, :] for ka in range(n_ka)], axis=0)
    )
    factor_a = solved_a * row
    factor_a_ref[...] = factor_a
    summed = unpack(total) * row
    solved_b = dot(summed, unpack(inverse(pack(gram_a * gram_c_ref[...]))))
    solved_b_ref[...] = solved_b
    gram_b = pack(dot(solved_b, solved_b, ((0,), (0,))))
    a_low = factor_a.astype(BF16).T
    b_turned = solved_b.T
    part = jnp.zeros((R, turned_ref.shape[2]), F32)
    for j in range(turned_ref.shape[0]):
        along = jnp.dot(a_low, turned_ref[j], preferred_element_type=F32)
        part += along * b_turned[:, j : j + 1]
    half = R // 2
    first = jnp.concatenate([part[:half], gram_b], axis=0)
    second = jnp.concatenate([part[half:], gram_b], axis=0)
    for n in range(n_ja // 2):
        send_ref[2 * n] = first
        send_ref[2 * n + 1] = second


def pass_kernel(got_ref, send_ref, gram_ref):
    total = jnp.sum(got_ref[...], axis=0)
    half = R // 2
    gram_ref[...] = total[half:]
    send_ref[...] = jnp.broadcast_to(total[None, :half], send_ref.shape)


def last_weights_kernel(totals, sizes, place_ref, gram_b_ref, gram_a_ref, factor_a_ref, solved_b_ref,
                        weights_ref, out_a_ref, out_b_ref):
    n_ia, n_ja, n_ka = sizes
    ia, ja, ka = place_ref[0], place_ref[1], place_ref[2]
    gram_raw = unpack(gram_b_ref[...])
    row, column = scales(gram_raw, totals[1])
    gram_b = gram_raw * row * column
    out_a_ref[...] = factor_a_ref[pl.ds(ja * n_ka + ka, 1), :]
    out_b_ref[...] = solved_b_ref[pl.ds(ia * n_ka + ka, 1), :] * row
    weights_ref[...] = unpack(inverse(pack(gram_a_ref[...] * gram_b))) * row


def fourth_kernel(sizes, place_ref, got_ref, weights_ref, send_ref, own_c_ref):
    n_ia, n_ja, n_ka = sizes
    ia, ja = place_ref[0], place_ref[1]
    first = got_ref[0]
    second = got_ref[1]
    for n in range(1, n_ia):
        first += got_ref[2 * n]
        second += got_ref[2 * n + 1]
    solved = dot(weights_ref[...], jnp.concatenate([first, second], axis=0))
    squares = dot(jnp.ones((8, solved.shape[1]), F32), solved * solved, ((1,), (1,)))
    squares = jnp.concatenate([squares, jnp.zeros((8, LANES - R), F32)], axis=1)
    send_ref[...] = jnp.broadcast_to(squares[None], send_ref.shape)
    k_of = lax.broadcasted_iota(jnp.int32, (8, solved.shape[1]), 1)
    t_of = lax.broadcasted_iota(jnp.int32, (8, solved.shape[1]), 0)
    chosen = jnp.where(k_of == 2 * (ia * n_ja + ja) + t_of, 1.0, 0.0)
    own_c_ref[...] = dot(chosen, solved, ((1,), (1,)))


def last_kernel(total, got_ref, own_c_ref, out_ref):
    squares = jnp.sum(got_ref[...], axis=0)[0:1, 0:R]
    out_ref[...] = own_c_ref[0:2, :] * lax.rsqrt(squares / total + 1e-06)


def exchange(blocks, axes, groups=None):
    return lax.all_to_all(blocks, axes, 0, 0, tiled=True, axis_index_groups=groups)


def local(tensor, factor_b, factor_c):
    rows_i, rows_j, rows_k = tensor.shape
    sizes = tuple(lax.axis_size(axis) for axis in ("ia", "ja", "ka"))
    n_ia, n_ja, n_ka = sizes
    totals = (rows_i * n_ia, rows_j * n_ja, rows_k * n_ka)
    cores = 2
    low_i = rows_i // (PACK * n_ka)
    place = jnp.stack([lax.axis_index(axis) for axis in ("ia", "ja", "ka")]).astype(jnp.int32)
    line = [
        [x * n_ja + z * cores + core for x in range(n_ia) for core in range(cores)]
        for z in range(n_ja // cores)
    ]
    (send,) = call(own_kernel, [shape(n_ia * n_ja, LANES)], [factor_b[0], factor_c[0]], 2**10)
    rows = exchange(send, ("ia", "ja"))
    turned = jnp.transpose(tensor, (1, 0, 2))
    rows, turned = lax.optimization_barrier((rows, turned))
    (send,) = call(
        lambda *refs: along_kernel(sizes, *refs),
        [shape(n_ka, low_i * rows_j + 2 * SUB, LANES)],
        [place, rows, tensor],
        2**26,
        scalars=1,
    )
    got = exchange(send, "ka")
    send, along, grams = call(
        lambda *refs: first_kernel(low_i, *refs),
        [shape(n_ja, 8, LANES), shape(low_i * rows_j, LANES), shape(2 * SUB, LANES)],
        [got],
        2**20,
    )
    got = exchange(send, "ja")
    weights_a, gram_c = call(weights_kernel, [shape(LANES, LANES), shape(R, R)], [grams], 2**24)
    (send,) = call(
        lambda *refs: second_kernel(low_i, *refs),
        [shape(n_ia * n_ka, SUB + low_i, LANES)],
        [got, weights_a, along],
        2**20,
    )
    got = exchange(send, ("ia", "ka"))
    send, gram_a, factor_a, solved_b = call(
        lambda *refs: third_kernel(totals, sizes, *refs),
        [
            shape(n_ja, R // 2 + SUB, LANES),
            shape(R, R),
            shape(rows_i, R),
            shape(rows_j, R),
        ],
        [place, got, gram_c, turned],
        2**26,
        scalars=1,
    )
    got = exchange(send, "ja")
    send, gram_b = call(
        pass_kernel, [shape(n_ia * cores, R // 2, LANES), shape(SUB, LANES)], [got], 2**16
    )
    got = exchange(send, ("ia", "ja"), line)
    weights_c, out_a, out_b = call(
        lambda *refs: last_weights_kernel(totals, sizes, *refs),
        [shape(R, R), shape(1, R), shape(1, R)],
        [place, gram_b, gram_a, factor_a, solved_b],
        2**24,
        scalars=1,
    )
    send, own_c = call(
        lambda *refs: fourth_kernel(sizes, *refs),
        [shape(n_ka, 8, LANES), shape(8, R)],
        [place, got, weights_c],
        2**20,
        scalars=1,
    )
    got = exchange(send, "ka")
    (out_c,) = call(
        lambda *refs: last_kernel(totals[2], *refs), [shape(2, R)], [got, own_c], 2**12
    )
    return out_a[None], out_b[None], out_c[None]


def solution(mesh):
    placed = (P("ia", "ja", "ka"), P("ja", ("ia", "ka"), None), P("ka", ("ia", "ja"), None))
    return jax.shard_map(
        local,
        mesh=mesh,
        in_specs=placed,
        out_specs=(
            P("ia", ("ja", "ka"), None),
            P("ja", ("ia", "ka"), None),
            P("ka", ("ia", "ja"), None),
        ),
        check_vma=False,
    )
```

```python
import jax
import jax.numpy as jnp
from jax import lax
from jax.experimental import pallas as pl
from jax.experimental.pallas import tpu as pltpu
from jax.sharding import PartitionSpec as P

HIGH = lax.Precision.HIGHEST
F32 = jnp.float32
BF16 = jnp.bfloat16
R = 32
LANES = 128
PACK = LANES // R
SUB = R // PACK


def dot(left, right, dims=((1,), (0,))):
    return lax.dot_general(
        left, right, (dims, ((), ())), precision=HIGH, preferred_element_type=F32
    )


def pack(matrix):
    rows = matrix.shape[0] // PACK
    return jnp.concatenate([matrix[g * rows : (g + 1) * rows] for g in range(PACK)], axis=1)


def unpack(packed):
    return jnp.concatenate([packed[:, g * R : (g + 1) * R] for g in range(PACK)], axis=0)


def lane_groups(matrix):
    total = matrix[0:R, 0:R]
    for g in range(1, PACK):
        total += matrix[g * R : (g + 1) * R, g * R : (g + 1) * R]
    return total


def eye():
    rows = lax.broadcasted_iota(jnp.int32, (R, R), 0)
    cols = lax.broadcasted_iota(jnp.int32, (R, R), 1)
    return (rows == cols).astype(F32)


def inverse(packed):
    work = packed
    lane = lax.broadcasted_iota(jnp.int32, (SUB, LANES), 1)
    sub = lax.broadcasted_iota(jnp.int32, (SUB, LANES), 0)
    group, place = lane // R, lane % R
    for p in range(PACK):
        in_rows = group == p
        in_cols = place // SUB == p
        spread = [jnp.broadcast_to(work[s : s + 1, :], (SUB, LANES)) for s in range(SUB)]
        cols = [
            jnp.where(
                in_rows,
                jnp.where(sub == s, -1.0, 0.0),
                jnp.take_along_axis(work, group * R + p * SUB + s, axis=1),
            )
            for s in range(SUB)
        ]
        rows = [
            jnp.where(
                in_cols,
                jnp.where(place == p * SUB + s, 1.0, 0.0),
                jnp.take_along_axis(spread[s], p * R + place, axis=1),
            )
            for s in range(SUB)
        ]
        pivots = [[None] * SUB for _ in range(SUB)]
        for s in range(SUB):
            for t in range(s, SUB):
                where = jnp.full((SUB, LANES), p * R + p * SUB + t, jnp.int32)
                pivots[s][t] = pivots[t][s] = jnp.take_along_axis(spread[s], where, axis=1)
        for t in range(SUB):
            recip = 1.0 / pivots[t][t]
            rows[t] = rows[t] * recip
            for u in range(t + 1, SUB):
                pivots[t][u] = pivots[t][u] * recip
            for s in range(SUB):
                if s != t:
                    factor = pivots[s][t]
                    rows[s] = rows[s] - factor * rows[t]
                    for u in range(t + 1, SUB):
                        pivots[s][u] = pivots[s][u] - factor * pivots[t][u]
        work = jnp.where(in_rows | in_cols, 0.0, work)
        for col, row in zip(cols, rows):
            work = work - col * row
    return work


def scales(gram_raw, total):
    diagonal = gram_raw * eye()
    row = lax.rsqrt(jnp.sum(diagonal, axis=0, keepdims=True) / total + 1e-06)
    column = lax.rsqrt(jnp.sum(diagonal, axis=1, keepdims=True) / total + 1e-06)
    return row, column


def call(kernel, outs, args, flops, scalars=0, scratch=()):
    spec = [pl.BlockSpec(memory_space=pltpu.SMEM)] * scalars
    spec += [pl.BlockSpec(memory_space=pltpu.VMEM)] * (len(args) - scalars)
    moved = sum(4 * a.size for a in args) + sum(4 * o.size for o in outs)
    return pl.pallas_call(
        kernel,
        out_shape=outs,
        in_specs=spec,
        out_specs=[pl.BlockSpec(memory_space=pltpu.VMEM)] * len(outs),
        scratch_shapes=[pltpu.VMEM(dims, F32) for dims in scratch],
        compiler_params=pltpu.CompilerParams(vmem_limit_bytes=24 * 2**20),
        cost_estimate=pl.CostEstimate(flops=flops, bytes_accessed=moved, transcendentals=0),
    )(*args)


def shape(*dims, dtype=F32):
    return jax.ShapeDtypeStruct(dims, dtype)


def own_kernel(b_ref, c_ref, send_ref):
    row = jnp.concatenate(
        [b_ref[...], c_ref[0:1, :], c_ref[1:2, :], jnp.zeros((1, LANES - 3 * R), F32)], axis=1
    )
    send_ref[...] = jnp.broadcast_to(row, send_ref.shape)


def along_kernel(sizes, place_ref, rows_ref, tensor_ref, send_ref):
    n_ia, n_ja, n_ka = sizes
    rows_i, rows_j, rows_k = tensor_ref.shape
    ja = place_ref[1]
    rows = rows_ref[...]
    sources = rows.shape[0]
    k_of = lax.broadcasted_iota(jnp.int32, (rows_k, sources), 0)
    d_of = lax.broadcasted_iota(jnp.int32, (rows_k, sources), 1)
    low = rows.astype(BF16)
    even = jnp.where(k_of == 2 * d_of, 1.0, 0.0).astype(BF16)
    odd = jnp.where(k_of == 2 * d_of + 1, 1.0, 0.0).astype(BF16)
    block_c = jnp.dot(even, low[:, R : 2 * R], preferred_element_type=F32)
    block_c += jnp.dot(odd, low[:, 2 * R : 3 * R], preferred_element_type=F32)
    tiled = jnp.concatenate([block_c] * PACK, axis=1)
    lane = lax.broadcasted_iota(jnp.int32, (rows_k, LANES), 1) // R
    weights = jnp.concatenate(
        [jnp.where(lane == g, tiled, 0.0).astype(BF16) for g in range(PACK)], axis=0
    )
    low_i = rows_i // (PACK * n_ka)
    sums = low_i * rows_j
    for ka in range(n_ka):
        left = jnp.concatenate(
            [
                tensor_ref[(g * n_ka + ka) * low_i : (g * n_ka + ka + 1) * low_i].reshape(sums, rows_k)
                for g in range(PACK)
            ],
            axis=1,
        )
        send_ref[ka, 0:sums, :] = jnp.dot(left, weights, preferred_element_type=F32)
    products = dot(rows, rows, ((0,), (0,)))
    gram_b = products[0:R, 0:R]
    gram_c = products[R : 2 * R, R : 2 * R] + products[2 * R : 3 * R, 2 * R : 3 * R]
    own_b = jnp.concatenate(
        [rows_ref[pl.ds(ia * n_ja + ja, 1), 0:R] for ia in range(n_ia)], axis=1
    )
    upper = lax.broadcasted_iota(jnp.int32, (R, R), 0) <= lax.broadcasted_iota(jnp.int32, (R, R), 1)
    diagonal = jnp.sum(gram_c * eye(), axis=0, keepdims=True)
    riders = jnp.concatenate(
        [
            pack(jnp.where(upper, gram_b, gram_c)),
            own_b,
            jnp.concatenate([diagonal, jnp.zeros((1, LANES - R), F32)], axis=1),
            jnp.zeros((SUB - 2, LANES), F32),
        ],
        axis=0,
    )
    for ka in range(n_ka):
        send_ref[ka, sums:, :] = riders


def first_kernel(low_i, got_ref, send_ref, along_ref, weights_ref, gram_ref, grams_ref):
    sums = got_ref.shape[1] - 2 * SUB
    along = jnp.sum(got_ref[:, 0:sums, :], axis=0)
    along_ref[...] = along
    grams_ref[...] = jnp.sum(got_ref[:, sums:, :], axis=0)
    own_b = jnp.concatenate(
        [got_ref[ka, sums + SUB : sums + SUB + 1, :] for ka in range(got_ref.shape[0])], axis=0
    )
    block_b = unpack(own_b)
    rows_j = block_b.shape[0]
    wide_b = jnp.concatenate([block_b] * PACK, axis=1)
    terms = along.reshape(low_i, rows_j, LANES) * wide_b[None]
    summed = jnp.concatenate(
        [jnp.sum(terms, axis=1), jnp.zeros((8 - low_i, LANES), F32)], axis=0
    )
    send_ref[...] = jnp.broadcast_to(summed[None], send_ref.shape)
    first_weights(grams_ref, weights_ref, gram_ref)


def first_weights(grams_ref, weights_ref, gram_ref):
    mixed = unpack(grams_ref[0:SUB])
    turned = mixed.T
    rows = lax.broadcasted_iota(jnp.int32, (R, R), 0)
    cols = lax.broadcasted_iota(jnp.int32, (R, R), 1)
    gram_b = jnp.where(rows <= cols, mixed, turned)
    gram_c = jnp.where(rows > cols, mixed, jnp.where(rows == cols, grams_ref[SUB + 1 : SUB + 2, 0:R], turned))
    gram_ref[...] = gram_c
    one = unpack(inverse(pack(gram_b * gram_c)))
    tiled = jnp.concatenate([jnp.concatenate([one] * PACK, axis=1)] * PACK, axis=0)
    rows = lax.broadcasted_iota(jnp.int32, (LANES, LANES), 0) // R
    cols = lax.broadcasted_iota(jnp.int32, (LANES, LANES), 1) // R
    weights_ref[...] = jnp.where(rows == cols, tiled, 0.0)


def second_kernel(low_i, got_ref, weights_ref, along_ref, send_ref):
    summed = jnp.sum(got_ref[...], axis=0)
    solved = dot(summed, weights_ref[...])[0:low_i]
    rows_j = along_ref.shape[0] // low_i
    terms = along_ref[...].reshape(low_i, rows_j, LANES) * solved[:, None, :]
    wide = jnp.sum(terms, axis=0)
    part = wide[:, 0:R]
    for g in range(1, PACK):
        part += wide[:, g * R : (g + 1) * R]
    rows = jnp.concatenate([pack(part), solved] * 2, axis=0)
    for n in range(0, send_ref.shape[0], rows.shape[0]):
        send_ref[n : n + rows.shape[0], :] = rows


def third_kernel(
    totals, sizes, low_i, place_ref, got_ref, gram_c_ref, turned_ref,
    send_ref, gram_a_ref, factor_a_ref, solved_b_ref, everyone_ref,
):
    n_ia, n_ja, n_ka = sizes
    ia = place_ref[0]
    each = SUB + low_i
    pairs = got_ref.shape[0] // (2 * each)
    summed = jnp.sum(got_ref[...].reshape(pairs, 2 * each, LANES), axis=0)
    total = summed[0:SUB] + summed[each : each + SUB]
    lower = lax.broadcasted_iota(jnp.int32, (2 * low_i, LANES), 0) < low_i
    for n in range(pairs):
        start = 2 * each * n
        everyone_ref[2 * low_i * n : 2 * low_i * (n + 1), :] = jnp.where(
            lower,
            got_ref[start + SUB : start + 2 * SUB, :],
            got_ref[start + 2 * SUB : start + 3 * SUB, :],
        )
    everyone = everyone_ref[...]
    gram_raw = lane_groups(dot(everyone, everyone, ((0,), (0,))))
    row, column = scales(gram_raw, totals[0])
    gram_a = gram_raw * row * column
    gram_a_ref[...] = gram_a
    block = n_ka * low_i
    solved_a = unpack(everyone_ref[pl.ds(pl.multiple_of(ia * block, block), block), :])
    factor_a = solved_a * row
    factor_a_ref[...] = factor_a
    summed = unpack(total) * row
    solved_b = dot(summed, unpack(inverse(pack(gram_a * gram_c_ref[...]))))
    solved_b_ref[...] = solved_b
    gram_b = pack(dot(solved_b, solved_b, ((0,), (0,))))
    a_low = factor_a.astype(BF16).T
    b_turned = solved_b.T
    part = jnp.zeros((R, turned_ref.shape[2]), F32)
    for j in range(turned_ref.shape[0]):
        along = jnp.dot(a_low, turned_ref[j], preferred_element_type=F32)
        part += along * b_turned[:, j : j + 1]
    half = R // 2
    first = jnp.concatenate([part[:half], gram_b], axis=0)
    second = jnp.concatenate([part[half:], gram_b], axis=0)
    for n in range(n_ja // 2):
        send_ref[2 * n] = first
        send_ref[2 * n + 1] = second


def pass_kernel(got_ref, send_ref, gram_ref):
    total = jnp.sum(got_ref[...], axis=0)
    half = R // 2
    gram_ref[...] = total[half:]
    send_ref[...] = jnp.broadcast_to(total[None, :half], send_ref.shape)


def last_weights_kernel(totals, sizes, place_ref, gram_b_ref, gram_a_ref, factor_a_ref, solved_b_ref,
                        weights_ref, out_a_ref, out_b_ref):
    n_ia, n_ja, n_ka = sizes
    ia, ja, ka = place_ref[0], place_ref[1], place_ref[2]
    gram_raw = unpack(gram_b_ref[...])
    row, column = scales(gram_raw, totals[1])
    gram_b = gram_raw * row * column
    out_a_ref[...] = factor_a_ref[pl.ds(ja * n_ka + ka, 1), :]
    out_b_ref[...] = solved_b_ref[pl.ds(ia * n_ka + ka, 1), :] * row
    weights_ref[...] = unpack(inverse(pack(gram_a_ref[...] * gram_b))) * row


def fourth_kernel(sizes, place_ref, got_ref, weights_ref, send_ref, own_c_ref):
    n_ia, n_ja, n_ka = sizes
    ia, ja = place_ref[0], place_ref[1]
    first = got_ref[0]
    second = got_ref[1]
    for n in range(1, n_ia):
        first += got_ref[2 * n]
        second += got_ref[2 * n + 1]
    solved = dot(weights_ref[...], jnp.concatenate([first, second], axis=0))
    squares = dot(jnp.ones((8, solved.shape[1]), F32), solved * solved, ((1,), (1,)))
    squares = jnp.concatenate([squares, jnp.zeros((8, LANES - R), F32)], axis=1)
    send_ref[...] = jnp.broadcast_to(squares[None], send_ref.shape)
    k_of = lax.broadcasted_iota(jnp.int32, (8, solved.shape[1]), 1)
    t_of = lax.broadcasted_iota(jnp.int32, (8, solved.shape[1]), 0)
    chosen = jnp.where(k_of == 2 * (ia * n_ja + ja) + t_of, 1.0, 0.0)
    own_c_ref[...] = dot(chosen, solved, ((1,), (1,)))


def last_kernel(total, got_ref, own_c_ref, out_ref):
    squares = jnp.sum(got_ref[...], axis=0)[0:1, 0:R]
    out_ref[...] = own_c_ref[0:2, :] * lax.rsqrt(squares / total + 1e-06)


def exchange(blocks, axes, groups=None):
    return lax.all_to_all(blocks, axes, 0, 0, tiled=True, axis_index_groups=groups)


def local(tensor, factor_b, factor_c):
    rows_i, rows_j, rows_k = tensor.shape
    sizes = tuple(lax.axis_size(axis) for axis in ("ia", "ja", "ka"))
    n_ia, n_ja, n_ka = sizes
    totals = (rows_i * n_ia, rows_j * n_ja, rows_k * n_ka)
    cores = 2
    low_i = rows_i // (PACK * n_ka)
    place = jnp.stack([lax.axis_index(axis) for axis in ("ia", "ja", "ka")]).astype(jnp.int32)
    line = [
        [x * n_ja + z * cores + core for x in range(n_ia) for core in range(cores)]
        for z in range(n_ja // cores)
    ]
    (send,) = call(own_kernel, [shape(n_ia * n_ja, LANES)], [factor_b[0], factor_c[0]], 2**10)
    rows = exchange(send, ("ia", "ja"))
    turned = jnp.transpose(tensor, (1, 0, 2))
    rows, turned = lax.optimization_barrier((rows, turned))
    (send,) = call(
        lambda *refs: along_kernel(sizes, *refs),
        [shape(n_ka, low_i * rows_j + 2 * SUB, LANES)],
        [place, rows, tensor],
        2**26,
        scalars=1,
    )
    got = exchange(send, "ka")
    send, along, weights_a, gram_c = call(
        lambda *refs: first_kernel(low_i, *refs),
        [shape(n_ja, 8, LANES), shape(low_i * rows_j, LANES), shape(LANES, LANES), shape(R, R)],
        [got],
        2**20,
        scratch=[(2 * SUB, LANES)],
    )
    got = exchange(send, "ja")
    (send,) = call(
        lambda *refs: second_kernel(low_i, *refs),
        [shape(n_ia * n_ka * (SUB + low_i), LANES)],
        [got, weights_a, along],
        2**20,
    )
    got = exchange(send[:, None, :], ("ia", "ka"))[:, 0, :]
    send, gram_a, factor_a, solved_b = call(
        lambda *refs: third_kernel(totals, sizes, low_i, *refs),
        [
            shape(n_ja, R // 2 + SUB, LANES),
            shape(R, R),
            shape(rows_i, R),
            shape(rows_j, R),
        ],
        [place, got, gram_c, turned],
        2**26,
        scalars=1,
        scratch=[(n_ia * n_ka * low_i, LANES)],
    )
    got = exchange(send, "ja")
    send, gram_b = call(
        pass_kernel, [shape(n_ia * cores, R // 2, LANES), shape(SUB, LANES)], [got], 2**16
    )
    got = exchange(send, ("ia", "ja"), line)
    weights_c, out_a, out_b = call(
        lambda *refs: last_weights_kernel(totals, sizes, *refs),
        [shape(R, R), shape(1, R), shape(1, R)],
        [place, gram_b, gram_a, factor_a, solved_b],
        2**24,
        scalars=1,
    )
    send, own_c = call(
        lambda *refs: fourth_kernel(sizes, *refs),
        [shape(n_ka, 8, LANES), shape(8, R)],
        [place, got, weights_c],
        2**20,
        scalars=1,
    )
    got = exchange(send, "ka")
    (out_c,) = call(
        lambda *refs: last_kernel(totals[2], *refs), [shape(2, R)], [got, own_c], 2**12
    )
    return out_a[None], out_b[None], out_c[None]


def solution(mesh):
    placed = (P("ia", "ja", "ka"), P("ja", ("ia", "ka"), None), P("ka", ("ia", "ja"), None))
    return jax.shard_map(
        local,
        mesh=mesh,
        in_specs=placed,
        out_specs=(
            P("ia", ("ja", "ka"), None),
            P("ja", ("ia", "ka"), None),
            P("ka", ("ia", "ja"), None),
        ),
        check_vma=False,
    )
```

```python
import jax
import jax.numpy as jnp
from jax import lax
from jax.experimental import pallas as pl
from jax.experimental.pallas import tpu as pltpu
from jax.sharding import PartitionSpec as P

HIGH = lax.Precision.HIGHEST
F32 = jnp.float32
BF16 = jnp.bfloat16
R = 32
LANES = 128
PACK = LANES // R
SUB = R // PACK


def dot(left, right, dims=((1,), (0,))):
    return lax.dot_general(
        left, right, (dims, ((), ())), precision=HIGH, preferred_element_type=F32
    )


def pack(matrix):
    rows = matrix.shape[0] // PACK
    return jnp.concatenate([matrix[g * rows : (g + 1) * rows] for g in range(PACK)], axis=1)


def unpack(packed):
    return jnp.concatenate([packed[:, g * R : (g + 1) * R] for g in range(PACK)], axis=0)


def lane_groups(matrix):
    total = matrix[0:R, 0:R]
    for g in range(1, PACK):
        total += matrix[g * R : (g + 1) * R, g * R : (g + 1) * R]
    return total


def eye():
    rows = lax.broadcasted_iota(jnp.int32, (R, R), 0)
    cols = lax.broadcasted_iota(jnp.int32, (R, R), 1)
    return (rows == cols).astype(F32)


def inverse(packed):
    work = packed
    lane = lax.broadcasted_iota(jnp.int32, (SUB, LANES), 1)
    sub = lax.broadcasted_iota(jnp.int32, (SUB, LANES), 0)
    group, place = lane // R, lane % R
    for p in range(PACK):
        in_rows = group == p
        in_cols = place // SUB == p
        spread = [jnp.broadcast_to(work[s : s + 1, :], (SUB, LANES)) for s in range(SUB)]
        cols = [
            jnp.where(
                in_rows,
                jnp.where(sub == s, -1.0, 0.0),
                jnp.take_along_axis(work, group * R + p * SUB + s, axis=1),
            )
            for s in range(SUB)
        ]
        rows = [
            jnp.where(
                in_cols,
                jnp.where(place == p * SUB + s, 1.0, 0.0),
                jnp.take_along_axis(spread[s], p * R + place, axis=1),
            )
            for s in range(SUB)
        ]
        pivots = [[None] * SUB for _ in range(SUB)]
        for s in range(SUB):
            for t in range(s, SUB):
                where = jnp.full((SUB, LANES), p * R + p * SUB + t, jnp.int32)
                pivots[s][t] = pivots[t][s] = jnp.take_along_axis(spread[s], where, axis=1)
        for t in range(SUB):
            recip = 1.0 / pivots[t][t]
            rows[t] = rows[t] * recip
            for u in range(t + 1, SUB):
                pivots[t][u] = pivots[t][u] * recip
            for s in range(SUB):
                if s != t:
                    factor = pivots[s][t]
                    rows[s] = rows[s] - factor * rows[t]
                    for u in range(t + 1, SUB):
                        pivots[s][u] = pivots[s][u] - factor * pivots[t][u]
        work = jnp.where(in_rows | in_cols, 0.0, work)
        for col, row in zip(cols, rows):
            work = work - col * row
    return work


def scales(gram_raw, total):
    diagonal = gram_raw * eye()
    row = lax.rsqrt(jnp.sum(diagonal, axis=0, keepdims=True) / total + 1e-06)
    column = lax.rsqrt(jnp.sum(diagonal, axis=1, keepdims=True) / total + 1e-06)
    return row, column


def call(kernel, outs, args, flops, scalars=0, scratch=()):
    spec = [pl.BlockSpec(memory_space=pltpu.SMEM)] * scalars
    spec += [pl.BlockSpec(memory_space=pltpu.VMEM)] * (len(args) - scalars)
    moved = sum(4 * a.size for a in args) + sum(4 * o.size for o in outs)
    return pl.pallas_call(
        kernel,
        out_shape=outs,
        in_specs=spec,
        out_specs=[pl.BlockSpec(memory_space=pltpu.VMEM)] * len(outs),
        scratch_shapes=[pltpu.VMEM(dims, F32) for dims in scratch],
        compiler_params=pltpu.CompilerParams(vmem_limit_bytes=24 * 2**20),
        cost_estimate=pl.CostEstimate(flops=flops, bytes_accessed=moved, transcendentals=0),
    )(*args)


def shape(*dims, dtype=F32):
    return jax.ShapeDtypeStruct(dims, dtype)


def own_kernel(b_ref, c_ref, send_ref):
    row = jnp.concatenate(
        [b_ref[...], c_ref[0:1, :], c_ref[1:2, :], jnp.zeros((1, LANES - 3 * R), F32)], axis=1
    )
    send_ref[...] = jnp.broadcast_to(row, send_ref.shape)


def along_kernel(sizes, place_ref, rows_ref, tensor_ref, send_ref):
    n_ia, n_ja, n_ka = sizes
    rows_i, rows_j, rows_k = tensor_ref.shape
    ja = place_ref[1]
    rows = rows_ref[...]
    sources = rows.shape[0]
    k_of = lax.broadcasted_iota(jnp.int32, (rows_k, sources), 0)
    d_of = lax.broadcasted_iota(jnp.int32, (rows_k, sources), 1)
    low = rows.astype(BF16)
    even = jnp.where(k_of == 2 * d_of, 1.0, 0.0).astype(BF16)
    odd = jnp.where(k_of == 2 * d_of + 1, 1.0, 0.0).astype(BF16)
    block_c = jnp.dot(even, low[:, R : 2 * R], preferred_element_type=F32)
    block_c += jnp.dot(odd, low[:, 2 * R : 3 * R], preferred_element_type=F32)
    tiled = jnp.concatenate([block_c] * PACK, axis=1)
    lane = lax.broadcasted_iota(jnp.int32, (rows_k, LANES), 1) // R
    weights = jnp.concatenate(
        [jnp.where(lane == g, tiled, 0.0).astype(BF16) for g in range(PACK)], axis=0
    )
    group_i = rows_i // PACK
    sums = group_i // n_ka * rows_j
    left = jnp.concatenate(
        [
            tensor_ref[g * group_i : (g + 1) * group_i].reshape(group_i * rows_j, rows_k)
            for g in range(PACK)
        ],
        axis=1,
    )
    product = jnp.dot(left, weights, preferred_element_type=F32)
    send_ref[:, 0:sums, :] = product.reshape(n_ka, sums, LANES)
    products = dot(rows, rows, ((0,), (0,)))
    gram_b = products[0:R, 0:R]
    gram_c = products[R : 2 * R, R : 2 * R] + products[2 * R : 3 * R, 2 * R : 3 * R]
    own_b = jnp.concatenate(
        [rows_ref[pl.ds(ia * n_ja + ja, 1), 0:R] for ia in range(n_ia)], axis=1
    )
    upper = lax.broadcasted_iota(jnp.int32, (R, R), 0) <= lax.broadcasted_iota(jnp.int32, (R, R), 1)
    diagonal = jnp.sum(gram_c * eye(), axis=0, keepdims=True)
    riders = jnp.concatenate(
        [
            pack(jnp.where(upper, gram_b, gram_c)),
            own_b,
            jnp.concatenate([diagonal, jnp.zeros((1, LANES - R), F32)], axis=1),
            jnp.zeros((SUB - 2, LANES), F32),
        ],
        axis=0,
    )
    for ka in range(n_ka):
        send_ref[ka, sums:, :] = riders


def first_kernel(low_i, got_ref, send_ref, along_ref, weights_ref, gram_ref, grams_ref):
    sums = got_ref.shape[1] - 2 * SUB
    along = jnp.sum(got_ref[:, 0:sums, :], axis=0)
    along_ref[...] = along
    grams_ref[...] = jnp.sum(got_ref[:, sums:, :], axis=0)
    own_b = jnp.concatenate(
        [got_ref[ka, sums + SUB : sums + SUB + 1, :] for ka in range(got_ref.shape[0])], axis=0
    )
    block_b = unpack(own_b)
    rows_j = block_b.shape[0]
    wide_b = jnp.concatenate([block_b] * PACK, axis=1)
    terms = along.reshape(low_i, rows_j, LANES) * wide_b[None]
    summed = jnp.concatenate(
        [jnp.sum(terms, axis=1), jnp.zeros((8 - low_i, LANES), F32)], axis=0
    )
    send_ref[...] = jnp.broadcast_to(summed[None], send_ref.shape)
    first_weights(grams_ref, weights_ref, gram_ref)


def first_weights(grams_ref, weights_ref, gram_ref):
    mixed = unpack(grams_ref[0:SUB])
    turned = mixed.T
    rows = lax.broadcasted_iota(jnp.int32, (R, R), 0)
    cols = lax.broadcasted_iota(jnp.int32, (R, R), 1)
    gram_b = jnp.where(rows <= cols, mixed, turned)
    gram_c = jnp.where(rows > cols, mixed, jnp.where(rows == cols, grams_ref[SUB + 1 : SUB + 2, 0:R], turned))
    gram_ref[...] = gram_c
    one = unpack(inverse(pack(gram_b * gram_c)))
    tiled = jnp.concatenate([jnp.concatenate([one] * PACK, axis=1)] * PACK, axis=0)
    rows = lax.broadcasted_iota(jnp.int32, (LANES, LANES), 0) // R
    cols = lax.broadcasted_iota(jnp.int32, (LANES, LANES), 1) // R
    weights_ref[...] = jnp.where(rows == cols, tiled, 0.0)


def second_kernel(low_i, got_ref, weights_ref, along_ref, send_ref):
    summed = jnp.sum(got_ref[...], axis=0)
    solved = dot(summed, weights_ref[...])[0:low_i]
    rows_j = along_ref.shape[0] // low_i
    terms = along_ref[...].reshape(low_i, rows_j, LANES) * solved[:, None, :]
    wide = jnp.sum(terms, axis=0)
    part = wide[:, 0:R]
    for g in range(1, PACK):
        part += wide[:, g * R : (g + 1) * R]
    rows = jnp.concatenate([pack(part), solved] * 2, axis=0)
    for n in range(0, send_ref.shape[0], rows.shape[0]):
        send_ref[n : n + rows.shape[0], :] = rows


def third_kernel(
    totals, sizes, low_i, place_ref, got_ref, gram_c_ref, turned_ref,
    send_ref, gram_a_ref, factor_a_ref, solved_b_ref, everyone_ref,
):
    n_ia, n_ja, n_ka = sizes
    ia = place_ref[0]
    each = SUB + low_i
    pairs = got_ref.shape[0] // (2 * each)
    summed = jnp.sum(got_ref[...].reshape(pairs, 2 * each, LANES), axis=0)
    total = summed[0:SUB] + summed[each : each + SUB]
    lower = lax.broadcasted_iota(jnp.int32, (2 * low_i, LANES), 0) < low_i
    for n in range(pairs):
        start = 2 * each * n
        everyone_ref[2 * low_i * n : 2 * low_i * (n + 1), :] = jnp.where(
            lower,
            got_ref[start + SUB : start + 2 * SUB, :],
            got_ref[start + 2 * SUB : start + 3 * SUB, :],
        )
    everyone = everyone_ref[...]
    gram_raw = lane_groups(dot(everyone, everyone, ((0,), (0,))))
    row, column = scales(gram_raw, totals[0])
    gram_a = gram_raw * row * column
    gram_a_ref[...] = gram_a
    block = n_ka * low_i
    solved_a = unpack(everyone_ref[pl.ds(pl.multiple_of(ia * block, block), block), :])
    factor_a = solved_a * row
    factor_a_ref[...] = factor_a
    summed = (unpack(total) * row).T
    solved_b = dot(unpack(inverse(pack(gram_a * gram_c_ref[...]))), summed)
    solved_b_ref[...] = solved_b
    gram_b = pack(dot(solved_b, solved_b, ((1,), (1,))))
    a_low = factor_a.astype(BF16).T
    part = jnp.zeros((R, turned_ref.shape[2]), F32)
    rows_j, rows_k = turned_ref.shape[0], turned_ref.shape[2]
    step = 8
    for start in range(0, rows_j, step):
        right = jnp.concatenate([turned_ref[start + j] for j in range(step)], axis=1)
        along = jnp.dot(a_low, right, preferred_element_type=F32)
        for j in range(step):
            part += along[:, j * rows_k : (j + 1) * rows_k] * solved_b[:, start + j : start + j + 1]
    half = R // 2
    first = jnp.concatenate([part[:half], gram_b], axis=0)
    second = jnp.concatenate([part[half:], gram_b], axis=0)
    for n in range(n_ja // 2):
        send_ref[2 * n] = first
        send_ref[2 * n + 1] = second


def pass_kernel(got_ref, send_ref, gram_ref):
    total = jnp.sum(got_ref[...], axis=0)
    half = R // 2
    gram_ref[...] = total[half:]
    send_ref[...] = jnp.broadcast_to(total[None, :half], send_ref.shape)


def last_weights_kernel(totals, sizes, place_ref, gram_b_ref, gram_a_ref, factor_a_ref, solved_b_ref,
                        weights_ref, out_a_ref, out_b_ref):
    n_ia, n_ja, n_ka = sizes
    ia, ja, ka = place_ref[0], place_ref[1], place_ref[2]
    gram_raw = unpack(gram_b_ref[...])
    row, column = scales(gram_raw, totals[1])
    gram_b = gram_raw * row * column
    out_a_ref[...] = factor_a_ref[pl.ds(ja * n_ka + ka, 1), :]
    solved_b = solved_b_ref[...]
    j_of = lax.broadcasted_iota(jnp.int32, (8, solved_b.shape[1]), 1)
    chosen = jnp.where(j_of == ia * n_ka + ka, 1.0, 0.0)
    out_b_ref[...] = dot(chosen, solved_b, ((1,), (1,)))[0:1] * row
    weights_ref[...] = unpack(inverse(pack(gram_a_ref[...] * gram_b))) * column


def fourth_kernel(sizes, place_ref, got_ref, weights_ref, send_ref, own_c_ref, solved_ref):
    n_ia, n_ja, n_ka = sizes
    ia, ja = place_ref[0], place_ref[1]
    first = got_ref[0]
    second = got_ref[1]
    for n in range(1, n_ia):
        first += got_ref[2 * n]
        second += got_ref[2 * n + 1]
    solved = dot(jnp.concatenate([first, second], axis=0).T, weights_ref[...])
    solved_ref[...] = solved
    squares = jnp.sum(solved * solved, axis=0, keepdims=True)
    squares = jnp.concatenate([squares, jnp.zeros((1, LANES - R), F32)], axis=1)
    send_ref[...] = jnp.broadcast_to(squares[None], send_ref.shape)
    own = 2 * (ia * n_ja + ja)
    own_c_ref[...] = jnp.concatenate(
        [solved_ref[pl.ds(own, 1), :], solved_ref[pl.ds(own + 1, 1), :]], axis=0
    )


def last_kernel(total, got_ref, own_c_ref, out_ref):
    squares = jnp.sum(got_ref[...], axis=0)[0:1, 0:R]
    out_ref[...] = own_c_ref[...] * lax.rsqrt(squares / total + 1e-06)


def exchange(blocks, axes, groups=None):
    return lax.all_to_all(blocks, axes, 0, 0, tiled=True, axis_index_groups=groups)


def local(tensor, factor_b, factor_c):
    rows_i, rows_j, rows_k = tensor.shape
    sizes = tuple(lax.axis_size(axis) for axis in ("ia", "ja", "ka"))
    n_ia, n_ja, n_ka = sizes
    totals = (rows_i * n_ia, rows_j * n_ja, rows_k * n_ka)
    cores = 2
    low_i = rows_i // (PACK * n_ka)
    place = jnp.stack([lax.axis_index(axis) for axis in ("ia", "ja", "ka")]).astype(jnp.int32)
    line = [
        [x * n_ja + z * cores + core for x in range(n_ia) for core in range(cores)]
        for z in range(n_ja // cores)
    ]
    (send,) = call(own_kernel, [shape(n_ia * n_ja, LANES)], [factor_b[0], factor_c[0]], 2**10)
    rows = exchange(send, ("ia", "ja"))
    turned = jnp.transpose(tensor, (1, 0, 2))
    rows, turned = lax.optimization_barrier((rows, turned))
    (send,) = call(
        lambda *refs: along_kernel(sizes, *refs),
        [shape(n_ka, low_i * rows_j + 2 * SUB, LANES)],
        [place, rows, tensor],
        2**26,
        scalars=1,
    )
    got = exchange(send, "ka")
    send, along, weights_a, gram_c = call(
        lambda *refs: first_kernel(low_i, *refs),
        [shape(n_ja, 8, LANES), shape(low_i * rows_j, LANES), shape(LANES, LANES), shape(R, R)],
        [got],
        2**20,
        scratch=[(2 * SUB, LANES)],
    )
    got = exchange(send, "ja")
    (send,) = call(
        lambda *refs: second_kernel(low_i, *refs),
        [shape(n_ia * n_ka * (SUB + low_i), LANES)],
        [got, weights_a, along],
        2**20,
    )
    got = exchange(send[:, None, :], ("ia", "ka"))[:, 0, :]
    send, gram_a, factor_a, solved_b = call(
        lambda *refs: third_kernel(totals, sizes, low_i, *refs),
        [
            shape(n_ja, R // 2 + SUB, LANES),
            shape(R, R),
            shape(rows_i, R),
            shape(R, rows_j),
        ],
        [place, got, gram_c, turned],
        2**26,
        scalars=1,
        scratch=[(n_ia * n_ka * low_i, LANES)],
    )
    got = exchange(send, "ja")
    send, gram_b = call(
        pass_kernel, [shape(n_ia * cores, R // 2, LANES), shape(SUB, LANES)], [got], 2**16
    )
    got = exchange(send, ("ia", "ja"), line)
    weights_c, out_a, out_b = call(
        lambda *refs: last_weights_kernel(totals, sizes, *refs),
        [shape(R, R), shape(1, R), shape(1, R)],
        [place, gram_b, gram_a, factor_a, solved_b],
        2**24,
        scalars=1,
    )
    send, own_c = call(
        lambda *refs: fourth_kernel(sizes, *refs),
        [shape(n_ka, 8, LANES), shape(2, R)],
        [place, got, weights_c],
        2**20,
        scalars=1,
        scratch=[(rows_k, R)],
    )
    got = exchange(send, "ka")
    (out_c,) = call(
        lambda *refs: last_kernel(totals[2], *refs), [shape(2, R)], [got, own_c], 2**12
    )
    return out_a[None], out_b[None], out_c[None]


def solution(mesh):
    placed = (P("ia", "ja", "ka"), P("ja", ("ia", "ka"), None), P("ka", ("ia", "ja"), None))
    return jax.shard_map(
        local,
        mesh=mesh,
        in_specs=placed,
        out_specs=(
            P("ia", ("ja", "ka"), None),
            P("ja", ("ia", "ka"), None),
            P("ka", ("ia", "ja"), None),
        ),
        check_vma=False,
    )
```

```python
import jax
import jax.numpy as jnp
from jax import lax
from jax.experimental import pallas as pl
from jax.experimental.pallas import tpu as pltpu
from jax.sharding import PartitionSpec as P

HIGH = lax.Precision.HIGHEST
F32 = jnp.float32
BF16 = jnp.bfloat16
R = 32
LANES = 128
PACK = LANES // R
SUB = R // PACK


def dot(left, right, dims=((1,), (0,))):
    return lax.dot_general(
        left, right, (dims, ((), ())), precision=HIGH, preferred_element_type=F32
    )


def pack(matrix):
    rows = matrix.shape[0] // PACK
    return jnp.concatenate([matrix[g * rows : (g + 1) * rows] for g in range(PACK)], axis=1)


def unpack(packed):
    return jnp.concatenate([packed[:, g * R : (g + 1) * R] for g in range(PACK)], axis=0)


def lane_groups(matrix):
    total = matrix[0:R, 0:R]
    for g in range(1, PACK):
        total += matrix[g * R : (g + 1) * R, g * R : (g + 1) * R]
    return total


def eye():
    rows = lax.broadcasted_iota(jnp.int32, (R, R), 0)
    cols = lax.broadcasted_iota(jnp.int32, (R, R), 1)
    return (rows == cols).astype(F32)


def inverse(packed):
    work = packed
    lane = lax.broadcasted_iota(jnp.int32, (SUB, LANES), 1)
    sub = lax.broadcasted_iota(jnp.int32, (SUB, LANES), 0)
    group, place = lane // R, lane % R
    for p in range(PACK):
        in_rows = group == p
        in_cols = place // SUB == p
        spread = [jnp.broadcast_to(work[s : s + 1, :], (SUB, LANES)) for s in range(SUB)]
        cols = [
            jnp.where(
                in_rows,
                jnp.where(sub == s, -1.0, 0.0),
                jnp.take_along_axis(work, group * R + p * SUB + s, axis=1),
            )
            for s in range(SUB)
        ]
        rows = [
            jnp.where(
                in_cols,
                jnp.where(place == p * SUB + s, 1.0, 0.0),
                jnp.take_along_axis(spread[s], p * R + place, axis=1),
            )
            for s in range(SUB)
        ]
        pivots = [[None] * SUB for _ in range(SUB)]
        for s in range(SUB):
            for t in range(s, SUB):
                where = jnp.full((SUB, LANES), p * R + p * SUB + t, jnp.int32)
                pivots[s][t] = pivots[t][s] = jnp.take_along_axis(spread[s], where, axis=1)
        for t in range(SUB):
            recip = 1.0 / pivots[t][t]
            rows[t] = rows[t] * recip
            for u in range(t + 1, SUB):
                pivots[t][u] = pivots[t][u] * recip
            for s in range(SUB):
                if s != t:
                    factor = pivots[s][t]
                    rows[s] = rows[s] - factor * rows[t]
                    for u in range(t + 1, SUB):
                        pivots[s][u] = pivots[s][u] - factor * pivots[t][u]
        work = jnp.where(in_rows | in_cols, 0.0, work)
        for col, row in zip(cols, rows):
            work = work - col * row
    return work


def scales(gram_raw, total):
    diagonal = gram_raw * eye()
    row = lax.rsqrt(jnp.sum(diagonal, axis=0, keepdims=True) / total + 1e-06)
    column = lax.rsqrt(jnp.sum(diagonal, axis=1, keepdims=True) / total + 1e-06)
    return row, column


def call(kernel, outs, args, flops, scalars=0, scratch=()):
    spec = [pl.BlockSpec(memory_space=pltpu.SMEM)] * scalars
    spec += [pl.BlockSpec(memory_space=pltpu.VMEM)] * (len(args) - scalars)
    moved = sum(4 * a.size for a in args) + sum(4 * o.size for o in outs)
    return pl.pallas_call(
        kernel,
        out_shape=outs,
        in_specs=spec,
        out_specs=[pl.BlockSpec(memory_space=pltpu.VMEM)] * len(outs),
        scratch_shapes=[pltpu.VMEM(dims, F32) for dims in scratch],
        compiler_params=pltpu.CompilerParams(vmem_limit_bytes=24 * 2**20),
        cost_estimate=pl.CostEstimate(flops=flops, bytes_accessed=moved, transcendentals=0),
    )(*args)


def shape(*dims, dtype=F32):
    return jax.ShapeDtypeStruct(dims, dtype)


def own_kernel(b_ref, c_ref, send_ref):
    row = jnp.concatenate(
        [b_ref[...], c_ref[0:1, :], c_ref[1:2, :], jnp.zeros((1, LANES - 3 * R), F32)], axis=1
    )
    send_ref[...] = jnp.broadcast_to(row, send_ref.shape)


def along_kernel(sizes, place_ref, rows_ref, tensor_ref, send_ref):
    n_ia, n_ja, n_ka = sizes
    rows_i, rows_j, rows_k = tensor_ref.shape
    ja = place_ref[1]
    rows = rows_ref[...]
    sources = rows.shape[0]
    k_of = lax.broadcasted_iota(jnp.int32, (rows_k, sources), 0)
    d_of = lax.broadcasted_iota(jnp.int32, (rows_k, sources), 1)
    low = rows.astype(BF16)
    even = jnp.where(k_of == 2 * d_of, 1.0, 0.0).astype(BF16)
    odd = jnp.where(k_of == 2 * d_of + 1, 1.0, 0.0).astype(BF16)
    block_c = jnp.dot(even, low[:, R : 2 * R], preferred_element_type=F32)
    block_c += jnp.dot(odd, low[:, 2 * R : 3 * R], preferred_element_type=F32)
    tiled = jnp.concatenate([block_c] * PACK, axis=1)
    lane = lax.broadcasted_iota(jnp.int32, (rows_k, LANES), 1) // R
    weights = jnp.concatenate(
        [jnp.where(lane == g, tiled, 0.0).astype(BF16) for g in range(PACK)], axis=0
    )
    group_i = rows_i // PACK
    sums = group_i // n_ka * rows_j
    left = jnp.concatenate(
        [
            tensor_ref[g * group_i : (g + 1) * group_i].reshape(group_i * rows_j, rows_k)
            for g in range(PACK)
        ],
        axis=1,
    )
    product = jnp.dot(left, weights, preferred_element_type=F32)
    send_ref[:, 0:sums, :] = product.astype(BF16).reshape(n_ka, sums, LANES)
    products = dot(rows, rows, ((0,), (0,)))
    gram_b = products[0:R, 0:R]
    gram_c = products[R : 2 * R, R : 2 * R] + products[2 * R : 3 * R, 2 * R : 3 * R]
    own_b = jnp.concatenate(
        [rows_ref[pl.ds(ia * n_ja + ja, 1), 0:R] for ia in range(n_ia)], axis=1
    )
    upper = lax.broadcasted_iota(jnp.int32, (R, R), 0) <= lax.broadcasted_iota(jnp.int32, (R, R), 1)
    diagonal = jnp.sum(gram_c * eye(), axis=0, keepdims=True)
    riders = jnp.concatenate(
        [
            pack(jnp.where(upper, gram_b, gram_c)),
            own_b,
            jnp.concatenate([diagonal, jnp.zeros((1, LANES - R), F32)], axis=1),
        ],
        axis=0,
    )
    high = riders.astype(BF16).astype(F32)
    middle = (riders - high).astype(BF16).astype(F32)
    low = riders - high - middle
    riders = jnp.concatenate([high, middle, low, jnp.zeros((2, LANES), F32)], axis=0).astype(BF16)
    for ka in range(n_ka):
        send_ref[ka, sums:, :] = riders


def first_kernel(low_i, got_ref, send_ref, along_ref, weights_ref, gram_ref, grams_ref):
    sums = got_ref.shape[1] - 4 * SUB
    n_ka = got_ref.shape[0]
    along = jnp.zeros((sums, LANES), F32)
    own_b = []
    total = jnp.zeros((SUB + 2, LANES), F32)
    for ka in range(n_ka):
        along += got_ref[ka, 0:sums, :].astype(F32)
        parts = got_ref[ka, sums:, :].astype(F32)
        size = SUB + 2
        riders = (parts[0:size] + parts[size : 2 * size]) + parts[2 * size : 3 * size]
        total += riders
        own_b.append(riders[SUB : SUB + 1])
    along_ref[...] = along
    grams_ref[...] = jnp.concatenate([total, jnp.zeros((SUB - 2, LANES), F32)], axis=0)
    own_b = jnp.concatenate(own_b, axis=0)
    block_b = unpack(own_b)
    rows_j = block_b.shape[0]
    wide_b = jnp.concatenate([block_b] * PACK, axis=1)
    terms = along.reshape(low_i, rows_j, LANES) * wide_b[None]
    summed = jnp.concatenate(
        [jnp.sum(terms, axis=1), jnp.zeros((8 - low_i, LANES), F32)], axis=0
    )
    send_ref[...] = jnp.broadcast_to(summed[None], send_ref.shape)
    first_weights(grams_ref, weights_ref, gram_ref)


def first_weights(grams_ref, weights_ref, gram_ref):
    mixed = unpack(grams_ref[0:SUB])
    turned = mixed.T
    rows = lax.broadcasted_iota(jnp.int32, (R, R), 0)
    cols = lax.broadcasted_iota(jnp.int32, (R, R), 1)
    gram_b = jnp.where(rows <= cols, mixed, turned)
    gram_c = jnp.where(rows > cols, mixed, jnp.where(rows == cols, grams_ref[SUB + 1 : SUB + 2, 0:R], turned))
    gram_ref[...] = gram_c
    one = unpack(inverse(pack(gram_b * gram_c)))
    tiled = jnp.concatenate([jnp.concatenate([one] * PACK, axis=1)] * PACK, axis=0)
    rows = lax.broadcasted_iota(jnp.int32, (LANES, LANES), 0) // R
    cols = lax.broadcasted_iota(jnp.int32, (LANES, LANES), 1) // R
    weights_ref[...] = jnp.where(rows == cols, tiled, 0.0)


def second_kernel(low_i, got_ref, weights_ref, along_ref, send_ref):
    summed = jnp.sum(got_ref[...], axis=0)
    solved = dot(summed, weights_ref[...])[0:low_i]
    rows_j = along_ref.shape[0] // low_i
    terms = along_ref[...].reshape(low_i, rows_j, LANES) * solved[:, None, :]
    wide = jnp.sum(terms, axis=0)
    part = wide[:, 0:R]
    for g in range(1, PACK):
        part += wide[:, g * R : (g + 1) * R]
    rows = jnp.concatenate([pack(part), solved] * 2, axis=0)
    for n in range(0, send_ref.shape[0], rows.shape[0]):
        send_ref[n : n + rows.shape[0], :] = rows


def third_kernel(
    totals, sizes, low_i, place_ref, got_ref, gram_c_ref, turned_ref,
    send_ref, gram_a_ref, factor_a_ref, solved_b_ref, everyone_ref,
):
    n_ia, n_ja, n_ka = sizes
    ia = place_ref[0]
    each = SUB + low_i
    pairs = got_ref.shape[0] // (2 * each)
    summed = jnp.sum(got_ref[...].reshape(pairs, 2 * each, LANES), axis=0)
    total = summed[0:SUB] + summed[each : each + SUB]
    lower = lax.broadcasted_iota(jnp.int32, (2 * low_i, LANES), 0) < low_i
    for n in range(pairs):
        start = 2 * each * n
        everyone_ref[2 * low_i * n : 2 * low_i * (n + 1), :] = jnp.where(
            lower,
            got_ref[start + SUB : start + 2 * SUB, :],
            got_ref[start + 2 * SUB : start + 3 * SUB, :],
        )
    everyone = everyone_ref[...]
    gram_raw = lane_groups(dot(everyone, everyone, ((0,), (0,))))
    row, column = scales(gram_raw, totals[0])
    gram_a = gram_raw * row * column
    gram_a_ref[...] = gram_a
    block = n_ka * low_i
    solved_a = unpack(everyone_ref[pl.ds(pl.multiple_of(ia * block, block), block), :])
    factor_a = solved_a * row
    factor_a_ref[...] = factor_a
    summed = (unpack(total) * row).T
    solved_b = dot(unpack(inverse(pack(gram_a * gram_c_ref[...]))), summed)
    solved_b_ref[...] = solved_b
    gram_b = pack(dot(solved_b, solved_b, ((1,), (1,))))
    a_low = factor_a.astype(BF16).T
    part = jnp.zeros((R, turned_ref.shape[2]), F32)
    rows_j, rows_k = turned_ref.shape[0], turned_ref.shape[2]
    step = 8
    for start in range(0, rows_j, step):
        right = jnp.concatenate([turned_ref[start + j] for j in range(step)], axis=1)
        along = jnp.dot(a_low, right, preferred_element_type=F32)
        for j in range(step):
            part += along[:, j * rows_k : (j + 1) * rows_k] * solved_b[:, start + j : start + j + 1]
    half = R // 2
    first = jnp.concatenate([part[:half], gram_b], axis=0)
    second = jnp.concatenate([part[half:], gram_b], axis=0)
    for n in range(n_ja // 2):
        send_ref[2 * n] = first
        send_ref[2 * n + 1] = second


def pass_kernel(got_ref, send_ref, gram_ref):
    total = jnp.sum(got_ref[...], axis=0)
    half = R // 2
    gram_ref[...] = total[half:]
    send_ref[...] = jnp.broadcast_to(total[None, :half], send_ref.shape)


def last_weights_kernel(totals, sizes, place_ref, gram_b_ref, gram_a_ref, factor_a_ref, solved_b_ref,
                        weights_ref, out_a_ref, out_b_ref):
    n_ia, n_ja, n_ka = sizes
    ia, ja, ka = place_ref[0], place_ref[1], place_ref[2]
    gram_raw = unpack(gram_b_ref[...])
    row, column = scales(gram_raw, totals[1])
    gram_b = gram_raw * row * column
    out_a_ref[...] = factor_a_ref[pl.ds(ja * n_ka + ka, 1), :]
    solved_b = solved_b_ref[...]
    j_of = lax.broadcasted_iota(jnp.int32, (8, solved_b.shape[1]), 1)
    chosen = jnp.where(j_of == ia * n_ka + ka, 1.0, 0.0)
    out_b_ref[...] = dot(chosen, solved_b, ((1,), (1,)))[0:1] * row
    weights_ref[...] = unpack(inverse(pack(gram_a_ref[...] * gram_b))) * column


def fourth_kernel(sizes, place_ref, got_ref, weights_ref, send_ref, own_c_ref, solved_ref):
    n_ia, n_ja, n_ka = sizes
    ia, ja = place_ref[0], place_ref[1]
    first = got_ref[0]
    second = got_ref[1]
    for n in range(1, n_ia):
        first += got_ref[2 * n]
        second += got_ref[2 * n + 1]
    solved = dot(jnp.concatenate([first, second], axis=0).T, weights_ref[...])
    solved_ref[...] = solved
    squares = jnp.sum(solved * solved, axis=0, keepdims=True)
    squares = jnp.concatenate([squares, jnp.zeros((1, LANES - R), F32)], axis=1)
    send_ref[...] = jnp.broadcast_to(squares[None], send_ref.shape)
    own = 2 * (ia * n_ja + ja)
    own_c_ref[...] = jnp.concatenate(
        [solved_ref[pl.ds(own, 1), :], solved_ref[pl.ds(own + 1, 1), :]], axis=0
    )


def last_kernel(total, got_ref, own_c_ref, out_ref):
    squares = jnp.sum(got_ref[...], axis=0)[0:1, 0:R]
    out_ref[...] = own_c_ref[...] * lax.rsqrt(squares / total + 1e-06)


def exchange(blocks, axes, groups=None):
    return lax.all_to_all(blocks, axes, 0, 0, tiled=True, axis_index_groups=groups)


def local(tensor, factor_b, factor_c):
    rows_i, rows_j, rows_k = tensor.shape
    sizes = tuple(lax.axis_size(axis) for axis in ("ia", "ja", "ka"))
    n_ia, n_ja, n_ka = sizes
    totals = (rows_i * n_ia, rows_j * n_ja, rows_k * n_ka)
    cores = 2
    low_i = rows_i // (PACK * n_ka)
    place = jnp.stack([lax.axis_index(axis) for axis in ("ia", "ja", "ka")]).astype(jnp.int32)
    line = [
        [x * n_ja + z * cores + core for x in range(n_ia) for core in range(cores)]
        for z in range(n_ja // cores)
    ]
    (send,) = call(own_kernel, [shape(n_ia * n_ja, LANES)], [factor_b[0], factor_c[0]], 2**10)
    rows = exchange(send, ("ia", "ja"))
    turned = jnp.transpose(tensor, (1, 0, 2))
    rows, turned = lax.optimization_barrier((rows, turned))
    (send,) = call(
        lambda *refs: along_kernel(sizes, *refs),
        [shape(n_ka, low_i * rows_j + 4 * SUB, LANES, dtype=BF16)],
        [place, rows, tensor],
        2**26,
        scalars=1,
    )
    got = exchange(send, "ka")
    send, along, weights_a, gram_c = call(
        lambda *refs: first_kernel(low_i, *refs),
        [shape(n_ja, 8, LANES), shape(low_i * rows_j, LANES), shape(LANES, LANES), shape(R, R)],
        [got],
        2**20,
        scratch=[(2 * SUB, LANES)],
    )
    got = exchange(send, "ja")
    (send,) = call(
        lambda *refs: second_kernel(low_i, *refs),
        [shape(n_ia * n_ka * (SUB + low_i), LANES)],
        [got, weights_a, along],
        2**20,
    )
    got = exchange(send[:, None, :], ("ia", "ka"))[:, 0, :]
    send, gram_a, factor_a, solved_b = call(
        lambda *refs: third_kernel(totals, sizes, low_i, *refs),
        [
            shape(n_ja, R // 2 + SUB, LANES),
            shape(R, R),
            shape(rows_i, R),
            shape(R, rows_j),
        ],
        [place, got, gram_c, turned],
        2**26,
        scalars=1,
        scratch=[(n_ia * n_ka * low_i, LANES)],
    )
    got = exchange(send, "ja")
    send, gram_b = call(
        pass_kernel, [shape(n_ia * cores, R // 2, LANES), shape(SUB, LANES)], [got], 2**16
    )
    got = exchange(send, ("ia", "ja"), line)
    weights_c, out_a, out_b = call(
        lambda *refs: last_weights_kernel(totals, sizes, *refs),
        [shape(R, R), shape(1, R), shape(1, R)],
        [place, gram_b, gram_a, factor_a, solved_b],
        2**24,
        scalars=1,
    )
    send, own_c = call(
        lambda *refs: fourth_kernel(sizes, *refs),
        [shape(n_ka, 8, LANES), shape(2, R)],
        [place, got, weights_c],
        2**20,
        scalars=1,
        scratch=[(rows_k, R)],
    )
    got = exchange(send, "ka")
    (out_c,) = call(
        lambda *refs: last_kernel(totals[2], *refs), [shape(2, R)], [got, own_c], 2**12
    )
    return out_a[None], out_b[None], out_c[None]


def solution(mesh):
    placed = (P("ia", "ja", "ka"), P("ja", ("ia", "ka"), None), P("ka", ("ia", "ja"), None))
    return jax.shard_map(
        local,
        mesh=mesh,
        in_specs=placed,
        out_specs=(
            P("ia", ("ja", "ka"), None),
            P("ja", ("ia", "ka"), None),
            P("ka", ("ia", "ja"), None),
        ),
        check_vma=False,
    )
```

```python
import jax
import jax.numpy as jnp
from jax import lax
from jax.experimental import pallas as pl
from jax.experimental.pallas import tpu as pltpu
from jax.sharding import PartitionSpec as P

HIGH = lax.Precision.HIGHEST
F32 = jnp.float32
BF16 = jnp.bfloat16
R = 32
LANES = 128
PACK = LANES // R
SUB = R // PACK


def dot(left, right, dims=((1,), (0,))):
    return lax.dot_general(
        left, right, (dims, ((), ())), precision=HIGH, preferred_element_type=F32
    )


def pack(matrix):
    rows = matrix.shape[0] // PACK
    return jnp.concatenate([matrix[g * rows : (g + 1) * rows] for g in range(PACK)], axis=1)


def unpack(packed):
    return jnp.concatenate([packed[:, g * R : (g + 1) * R] for g in range(PACK)], axis=0)


def lane_groups(matrix):
    total = matrix[0:R, 0:R]
    for g in range(1, PACK):
        total += matrix[g * R : (g + 1) * R, g * R : (g + 1) * R]
    return total


def eye():
    rows = lax.broadcasted_iota(jnp.int32, (R, R), 0)
    cols = lax.broadcasted_iota(jnp.int32, (R, R), 1)
    return (rows == cols).astype(F32)


def inverse(packed):
    work = packed
    lane = lax.broadcasted_iota(jnp.int32, (SUB, LANES), 1)
    sub = lax.broadcasted_iota(jnp.int32, (SUB, LANES), 0)
    group, place = lane // R, lane % R
    for p in range(PACK):
        in_rows = group == p
        in_cols = place // SUB == p
        spread = [jnp.broadcast_to(work[s : s + 1, :], (SUB, LANES)) for s in range(SUB)]
        cols = [
            jnp.where(
                in_rows,
                jnp.where(sub == s, -1.0, 0.0),
                jnp.take_along_axis(work, group * R + p * SUB + s, axis=1),
            )
            for s in range(SUB)
        ]
        rows = [
            jnp.where(
                in_cols,
                jnp.where(place == p * SUB + s, 1.0, 0.0),
                jnp.take_along_axis(spread[s], p * R + place, axis=1),
            )
            for s in range(SUB)
        ]
        pivots = [[None] * SUB for _ in range(SUB)]
        for s in range(SUB):
            for t in range(s, SUB):
                where = jnp.full((SUB, LANES), p * R + p * SUB + t, jnp.int32)
                pivots[s][t] = pivots[t][s] = jnp.take_along_axis(spread[s], where, axis=1)
        for t in range(SUB):
            recip = 1.0 / pivots[t][t]
            rows[t] = rows[t] * recip
            for u in range(t + 1, SUB):
                pivots[t][u] = pivots[t][u] * recip
            for s in range(SUB):
                if s != t:
                    factor = pivots[s][t]
                    rows[s] = rows[s] - factor * rows[t]
                    for u in range(t + 1, SUB):
                        pivots[s][u] = pivots[s][u] - factor * pivots[t][u]
        work = jnp.where(in_rows | in_cols, 0.0, work)
        for col, row in zip(cols, rows):
            work = work - col * row
    return work


def scales(gram_raw, total):
    diagonal = gram_raw * eye()
    row = lax.rsqrt(jnp.sum(diagonal, axis=0, keepdims=True) / total + 1e-06)
    column = lax.rsqrt(jnp.sum(diagonal, axis=1, keepdims=True) / total + 1e-06)
    return row, column


def call(kernel, outs, args, flops, scalars=0, scratch=()):
    spec = [pl.BlockSpec(memory_space=pltpu.SMEM)] * scalars
    spec += [pl.BlockSpec(memory_space=pltpu.VMEM)] * (len(args) - scalars)
    moved = sum(4 * a.size for a in args) + sum(4 * o.size for o in outs)
    return pl.pallas_call(
        kernel,
        out_shape=outs,
        in_specs=spec,
        out_specs=[pl.BlockSpec(memory_space=pltpu.VMEM)] * len(outs),
        scratch_shapes=[pltpu.VMEM(dims, F32) for dims in scratch],
        compiler_params=pltpu.CompilerParams(vmem_limit_bytes=24 * 2**20),
        cost_estimate=pl.CostEstimate(flops=flops, bytes_accessed=moved, transcendentals=0),
    )(*args)


def shape(*dims, dtype=F32):
    return jax.ShapeDtypeStruct(dims, dtype)


def own_kernel(b_ref, c_ref, send_ref):
    row = jnp.concatenate(
        [b_ref[...], c_ref[0:1, :], c_ref[1:2, :], jnp.zeros((1, LANES - 3 * R), F32)], axis=1
    )
    send_ref[...] = jnp.broadcast_to(row, send_ref.shape)


def along_kernel(sizes, place_ref, rows_ref, tensor_ref, send_ref):
    n_ia, n_ja, n_ka = sizes
    rows_i, rows_j, rows_k = tensor_ref.shape
    ja = place_ref[1]
    rows = rows_ref[...]
    sources = rows.shape[0]
    k_of = lax.broadcasted_iota(jnp.int32, (rows_k, sources), 0)
    d_of = lax.broadcasted_iota(jnp.int32, (rows_k, sources), 1)
    low = rows.astype(BF16)
    even = jnp.where(k_of == 2 * d_of, 1.0, 0.0).astype(BF16)
    odd = jnp.where(k_of == 2 * d_of + 1, 1.0, 0.0).astype(BF16)
    block_c = jnp.dot(even, low[:, R : 2 * R], preferred_element_type=F32)
    block_c += jnp.dot(odd, low[:, 2 * R : 3 * R], preferred_element_type=F32)
    tiled = jnp.concatenate([block_c] * PACK, axis=1)
    lane = lax.broadcasted_iota(jnp.int32, (rows_k, LANES), 1) // R
    weights = jnp.concatenate(
        [jnp.where(lane == g, tiled, 0.0).astype(BF16) for g in range(PACK)], axis=0
    )
    group_i = rows_i // PACK
    sums = group_i // n_ka * rows_j
    left = jnp.concatenate(
        [
            tensor_ref[g * group_i : (g + 1) * group_i].reshape(group_i * rows_j, rows_k)
            for g in range(PACK)
        ],
        axis=1,
    )
    product = jnp.dot(left, weights, preferred_element_type=F32)
    send_ref[:, 0:sums, :] = product.astype(BF16).reshape(n_ka, sums, LANES)
    products = dot(rows, rows, ((0,), (0,)))
    gram_b = products[0:R, 0:R]
    gram_c = products[R : 2 * R, R : 2 * R] + products[2 * R : 3 * R, 2 * R : 3 * R]
    own_b = jnp.concatenate(
        [rows_ref[pl.ds(ia * n_ja + ja, 1), 0:R] for ia in range(n_ia)], axis=1
    )
    upper = lax.broadcasted_iota(jnp.int32, (R, R), 0) <= lax.broadcasted_iota(jnp.int32, (R, R), 1)
    diagonal = jnp.sum(gram_c * eye(), axis=0, keepdims=True)
    riders = jnp.concatenate(
        [
            pack(jnp.where(upper, gram_b, gram_c)),
            own_b,
            jnp.concatenate([diagonal, jnp.zeros((1, LANES - R), F32)], axis=1),
        ],
        axis=0,
    )
    high = riders.astype(BF16).astype(F32)
    middle = (riders - high).astype(BF16).astype(F32)
    low = riders - high - middle
    riders = jnp.concatenate([high, middle, low, jnp.zeros((2, LANES), F32)], axis=0).astype(BF16)
    for ka in range(n_ka):
        send_ref[ka, sums:, :] = riders


def first_kernel(low_i, got_ref, send_ref, along_ref, weights_ref, gram_ref, grams_ref):
    sums = got_ref.shape[1] - 4 * SUB
    n_ka = got_ref.shape[0]
    along = jnp.zeros((sums, LANES), F32)
    own_b = []
    total = jnp.zeros((SUB + 2, LANES), F32)
    for ka in range(n_ka):
        along += got_ref[ka, 0:sums, :].astype(F32)
        parts = got_ref[ka, sums:, :].astype(F32)
        size = SUB + 2
        riders = (parts[0:size] + parts[size : 2 * size]) + parts[2 * size : 3 * size]
        total += riders
        own_b.append(riders[SUB : SUB + 1])
    along_ref[...] = along
    grams_ref[...] = jnp.concatenate([total, jnp.zeros((SUB - 2, LANES), F32)], axis=0)
    own_b = jnp.concatenate(own_b, axis=0)
    block_b = unpack(own_b)
    rows_j = block_b.shape[0]
    wide_b = jnp.concatenate([block_b] * PACK, axis=1)
    terms = along.reshape(low_i, rows_j, LANES) * wide_b[None]
    summed = jnp.sum(terms, axis=1)
    rows = jnp.concatenate([summed] * (SUB // low_i), axis=0)
    for start in range(0, send_ref.shape[0], SUB):
        send_ref[start : start + SUB, :] = rows
    first_weights(grams_ref, weights_ref, gram_ref)


def first_weights(grams_ref, weights_ref, gram_ref):
    mixed = unpack(grams_ref[0:SUB])
    turned = mixed.T
    rows = lax.broadcasted_iota(jnp.int32, (R, R), 0)
    cols = lax.broadcasted_iota(jnp.int32, (R, R), 1)
    gram_b = jnp.where(rows <= cols, mixed, turned)
    gram_c = jnp.where(rows > cols, mixed, jnp.where(rows == cols, grams_ref[SUB + 1 : SUB + 2, 0:R], turned))
    gram_ref[...] = gram_c
    one = unpack(inverse(pack(gram_b * gram_c)))
    tiled = jnp.concatenate([jnp.concatenate([one] * PACK, axis=1)] * PACK, axis=0)
    rows = lax.broadcasted_iota(jnp.int32, (LANES, LANES), 0) // R
    cols = lax.broadcasted_iota(jnp.int32, (LANES, LANES), 1) // R
    weights_ref[...] = jnp.where(rows == cols, tiled, 0.0)


def second_kernel(low_i, got_ref, weights_ref, along_ref, send_ref):
    wide = jnp.sum(got_ref[...].reshape(got_ref.shape[0] // SUB, SUB, LANES), axis=0)
    summed = wide[0:low_i]
    for start in range(low_i, SUB, low_i):
        summed += wide[start : start + low_i]
    solved = dot(summed, weights_ref[...])
    rows_j = along_ref.shape[0] // low_i
    terms = along_ref[...].reshape(low_i, rows_j, LANES) * solved[:, None, :]
    wide = jnp.sum(terms, axis=0)
    part = wide[:, 0:R]
    for g in range(1, PACK):
        part += wide[:, g * R : (g + 1) * R]
    rows = jnp.concatenate([pack(part), solved] * 2, axis=0)
    for n in range(0, send_ref.shape[0], rows.shape[0]):
        send_ref[n : n + rows.shape[0], :] = rows


def third_kernel(
    totals, sizes, low_i, place_ref, got_ref, gram_c_ref, turned_ref,
    send_ref, gram_a_ref, factor_a_ref, solved_b_ref, everyone_ref,
):
    n_ia, n_ja, n_ka = sizes
    ia = place_ref[0]
    each = SUB + low_i
    pairs = got_ref.shape[0] // (2 * each)
    summed = jnp.sum(got_ref[...].reshape(pairs, 2 * each, LANES), axis=0)
    total = summed[0:SUB] + summed[each : each + SUB]
    lower = lax.broadcasted_iota(jnp.int32, (2 * low_i, LANES), 0) < low_i
    for n in range(pairs):
        start = 2 * each * n
        everyone_ref[2 * low_i * n : 2 * low_i * (n + 1), :] = jnp.where(
            lower,
            got_ref[start + SUB : start + 2 * SUB, :],
            got_ref[start + 2 * SUB : start + 3 * SUB, :],
        )
    everyone = everyone_ref[...]
    gram_raw = lane_groups(dot(everyone, everyone, ((0,), (0,))))
    row, column = scales(gram_raw, totals[0])
    gram_a = gram_raw * row * column
    gram_a_ref[...] = gram_a
    block = n_ka * low_i
    solved_a = unpack(everyone_ref[pl.ds(pl.multiple_of(ia * block, block), block), :])
    factor_a = solved_a * row
    factor_a_ref[...] = factor_a
    summed = (unpack(total) * row).T
    solved_b = dot(unpack(inverse(pack(gram_a * gram_c_ref[...]))), summed)
    solved_b_ref[...] = solved_b
    gram_b = pack(dot(solved_b, solved_b, ((1,), (1,))))
    a_low = factor_a.astype(BF16).T
    part = jnp.zeros((R, turned_ref.shape[2]), F32)
    rows_j, rows_k = turned_ref.shape[0], turned_ref.shape[2]
    step = 8
    for start in range(0, rows_j, step):
        right = jnp.concatenate([turned_ref[start + j] for j in range(step)], axis=1)
        along = jnp.dot(a_low, right, preferred_element_type=F32)
        for j in range(step):
            part += along[:, j * rows_k : (j + 1) * rows_k] * solved_b[:, start + j : start + j + 1]
    half = R // 2
    first = jnp.concatenate([part[:half], gram_b], axis=0)
    second = jnp.concatenate([part[half:], gram_b], axis=0)
    for n in range(n_ja // 2):
        send_ref[2 * n] = first
        send_ref[2 * n + 1] = second


def pass_kernel(got_ref, send_ref, gram_ref):
    total = jnp.sum(got_ref[...], axis=0)
    half = R // 2
    gram_ref[...] = total[half:]
    send_ref[...] = jnp.broadcast_to(total[None, :half], send_ref.shape)


def last_weights_kernel(totals, sizes, place_ref, gram_b_ref, gram_a_ref, factor_a_ref, solved_b_ref,
                        weights_ref, out_a_ref, out_b_ref):
    n_ia, n_ja, n_ka = sizes
    ia, ja, ka = place_ref[0], place_ref[1], place_ref[2]
    gram_raw = unpack(gram_b_ref[...])
    row, column = scales(gram_raw, totals[1])
    gram_b = gram_raw * row * column
    out_a_ref[...] = factor_a_ref[pl.ds(ja * n_ka + ka, 1), :]
    solved_b = solved_b_ref[...]
    j_of = lax.broadcasted_iota(jnp.int32, (8, solved_b.shape[1]), 1)
    chosen = jnp.where(j_of == ia * n_ka + ka, 1.0, 0.0)
    out_b_ref[...] = dot(chosen, solved_b, ((1,), (1,)))[0:1] * row
    weights_ref[...] = unpack(inverse(pack(gram_a_ref[...] * gram_b))) * column


def fourth_kernel(sizes, place_ref, got_ref, weights_ref, send_ref, own_c_ref, solved_ref):
    n_ia, n_ja, n_ka = sizes
    ia, ja = place_ref[0], place_ref[1]
    first = got_ref[0]
    second = got_ref[1]
    for n in range(1, n_ia):
        first += got_ref[2 * n]
        second += got_ref[2 * n + 1]
    solved = dot(jnp.concatenate([first, second], axis=0).T, weights_ref[...])
    solved_ref[...] = solved
    squares = jnp.sum(solved * solved, axis=0, keepdims=True)
    squares = jnp.concatenate([squares, jnp.zeros((1, LANES - R), F32)], axis=1)
    send_ref[...] = jnp.broadcast_to(squares, send_ref.shape)
    own = 2 * (ia * n_ja + ja)
    own_c_ref[...] = jnp.concatenate(
        [solved_ref[pl.ds(own, 1), :], solved_ref[pl.ds(own + 1, 1), :]], axis=0
    )


def last_kernel(total, got_ref, own_c_ref, out_ref):
    squares = jnp.sum(got_ref[...], axis=0, keepdims=True)[:, 0:R]
    out_ref[...] = own_c_ref[...] * lax.rsqrt(squares / total + 1e-06)


def exchange(blocks, axes, groups=None):
    return lax.all_to_all(blocks, axes, 0, 0, tiled=True, axis_index_groups=groups)


def exchange_rows(rows, axes):
    return exchange(rows[:, None, :], axes)[:, 0, :]


def local(tensor, factor_b, factor_c):
    rows_i, rows_j, rows_k = tensor.shape
    sizes = tuple(lax.axis_size(axis) for axis in ("ia", "ja", "ka"))
    n_ia, n_ja, n_ka = sizes
    totals = (rows_i * n_ia, rows_j * n_ja, rows_k * n_ka)
    cores = 2
    low_i = rows_i // (PACK * n_ka)
    place = jnp.stack([lax.axis_index(axis) for axis in ("ia", "ja", "ka")]).astype(jnp.int32)
    line = [
        [x * n_ja + z * cores + core for x in range(n_ia) for core in range(cores)]
        for z in range(n_ja // cores)
    ]
    (send,) = call(own_kernel, [shape(n_ia * n_ja, LANES)], [factor_b[0], factor_c[0]], 2**10)
    rows = exchange(send, ("ia", "ja"))
    turned = jnp.transpose(tensor, (1, 0, 2))
    rows, turned = lax.optimization_barrier((rows, turned))
    (send,) = call(
        lambda *refs: along_kernel(sizes, *refs),
        [shape(n_ka, low_i * rows_j + 4 * SUB, LANES, dtype=BF16)],
        [place, rows, tensor],
        2**26,
        scalars=1,
    )
    got = exchange(send, "ka")
    send, along, weights_a, gram_c = call(
        lambda *refs: first_kernel(low_i, *refs),
        [shape(n_ja * low_i, LANES), shape(low_i * rows_j, LANES), shape(LANES, LANES), shape(R, R)],
        [got],
        2**20,
        scratch=[(2 * SUB, LANES)],
    )
    got = exchange_rows(send, "ja")
    (send,) = call(
        lambda *refs: second_kernel(low_i, *refs),
        [shape(n_ia * n_ka * (SUB + low_i), LANES)],
        [got, weights_a, along],
        2**20,
    )
    got = exchange_rows(send, ("ia", "ka"))
    send, gram_a, factor_a, solved_b = call(
        lambda *refs: third_kernel(totals, sizes, low_i, *refs),
        [
            shape(n_ja, R // 2 + SUB, LANES),
            shape(R, R),
            shape(rows_i, R),
            shape(R, rows_j),
        ],
        [place, got, gram_c, turned],
        2**26,
        scalars=1,
        scratch=[(n_ia * n_ka * low_i, LANES)],
    )
    got = exchange(send, "ja")
    send, gram_b = call(
        pass_kernel, [shape(n_ia * cores, R // 2, LANES), shape(SUB, LANES)], [got], 2**16
    )
    got = exchange(send, ("ia", "ja"), line)
    weights_c, out_a, out_b = call(
        lambda *refs: last_weights_kernel(totals, sizes, *refs),
        [shape(R, R), shape(1, R), shape(1, R)],
        [place, gram_b, gram_a, factor_a, solved_b],
        2**24,
        scalars=1,
    )
    send, own_c = call(
        lambda *refs: fourth_kernel(sizes, *refs),
        [shape(n_ka, LANES), shape(2, R)],
        [place, got, weights_c],
        2**20,
        scalars=1,
        scratch=[(rows_k, R)],
    )
    got = exchange_rows(send, "ka")
    (out_c,) = call(
        lambda *refs: last_kernel(totals[2], *refs), [shape(2, R)], [got, own_c], 2**12
    )
    return out_a[None], out_b[None], out_c[None]


def solution(mesh):
    placed = (P("ia", "ja", "ka"), P("ja", ("ia", "ka"), None), P("ka", ("ia", "ja"), None))
    return jax.shard_map(
        local,
        mesh=mesh,
        in_specs=placed,
        out_specs=(
            P("ia", ("ja", "ka"), None),
            P("ja", ("ia", "ka"), None),
            P("ka", ("ia", "ja"), None),
        ),
        check_vma=False,
    )
```

```python
import jax
import jax.numpy as jnp
from jax import lax
from jax.experimental import pallas as pl
from jax.experimental.pallas import tpu as pltpu
from jax.sharding import PartitionSpec as P

HIGH = lax.Precision.HIGHEST
F32 = jnp.float32
BF16 = jnp.bfloat16
R = 32
LANES = 128
PACK = LANES // R
SUB = R // PACK


def dot(left, right, dims=((1,), (0,))):
    return lax.dot_general(
        left, right, (dims, ((), ())), precision=HIGH, preferred_element_type=F32
    )


def pack(matrix):
    rows = matrix.shape[0] // PACK
    return jnp.concatenate([matrix[g * rows : (g + 1) * rows] for g in range(PACK)], axis=1)


def unpack(packed):
    return jnp.concatenate([packed[:, g * R : (g + 1) * R] for g in range(PACK)], axis=0)


def lane_groups(matrix):
    total = matrix[0:R, 0:R]
    for g in range(1, PACK):
        total += matrix[g * R : (g + 1) * R, g * R : (g + 1) * R]
    return total


def eye():
    rows = lax.broadcasted_iota(jnp.int32, (R, R), 0)
    cols = lax.broadcasted_iota(jnp.int32, (R, R), 1)
    return (rows == cols).astype(F32)


def inverse(packed):
    work = packed
    lane = lax.broadcasted_iota(jnp.int32, (SUB, LANES), 1)
    sub = lax.broadcasted_iota(jnp.int32, (SUB, LANES), 0)
    group, place = lane // R, lane % R
    for p in range(PACK):
        in_rows = group == p
        in_cols = place // SUB == p
        spread = [jnp.broadcast_to(work[s : s + 1, :], (SUB, LANES)) for s in range(SUB)]
        cols = [
            jnp.where(
                in_rows,
                jnp.where(sub == s, -1.0, 0.0),
                jnp.take_along_axis(work, group * R + p * SUB + s, axis=1),
            )
            for s in range(SUB)
        ]
        rows = [
            jnp.where(
                in_cols,
                jnp.where(place == p * SUB + s, 1.0, 0.0),
                jnp.take_along_axis(spread[s], p * R + place, axis=1),
            )
            for s in range(SUB)
        ]
        pivots = [[None] * SUB for _ in range(SUB)]
        for s in range(SUB):
            for t in range(s, SUB):
                where = jnp.full((SUB, LANES), p * R + p * SUB + t, jnp.int32)
                pivots[s][t] = pivots[t][s] = jnp.take_along_axis(spread[s], where, axis=1)
        for t in range(SUB):
            recip = 1.0 / pivots[t][t]
            rows[t] = rows[t] * recip
            for u in range(t + 1, SUB):
                pivots[t][u] = pivots[t][u] * recip
            for s in range(SUB):
                if s != t:
                    factor = pivots[s][t]
                    rows[s] = rows[s] - factor * rows[t]
                    for u in range(t + 1, SUB):
                        pivots[s][u] = pivots[s][u] - factor * pivots[t][u]
        work = jnp.where(in_rows | in_cols, 0.0, work)
        for col, row in zip(cols, rows):
            work = work - col * row
    return work


def scales(gram_raw, total):
    diagonal = gram_raw * eye()
    row = lax.rsqrt(jnp.sum(diagonal, axis=0, keepdims=True) / total + 1e-06)
    column = lax.rsqrt(jnp.sum(diagonal, axis=1, keepdims=True) / total + 1e-06)
    return row, column


def call(kernel, outs, args, flops, scalars=0, scratch=()):
    spec = [pl.BlockSpec(memory_space=pltpu.SMEM)] * scalars
    spec += [pl.BlockSpec(memory_space=pltpu.VMEM)] * (len(args) - scalars)
    moved = sum(4 * a.size for a in args) + sum(4 * o.size for o in outs)
    return pl.pallas_call(
        kernel,
        out_shape=outs,
        in_specs=spec,
        out_specs=[pl.BlockSpec(memory_space=pltpu.VMEM)] * len(outs),
        scratch_shapes=[pltpu.VMEM(dims, F32) for dims in scratch],
        compiler_params=pltpu.CompilerParams(vmem_limit_bytes=24 * 2**20),
        cost_estimate=pl.CostEstimate(flops=flops, bytes_accessed=moved, transcendentals=0),
    )(*args)


def shape(*dims, dtype=F32):
    return jax.ShapeDtypeStruct(dims, dtype)


def own_kernel(b_ref, c_ref, send_ref):
    row = jnp.concatenate(
        [b_ref[...], c_ref[0:1, :], c_ref[1:2, :], jnp.zeros((1, LANES - 3 * R), F32)], axis=1
    )
    send_ref[...] = jnp.broadcast_to(row, send_ref.shape)


def along_kernel(sizes, place_ref, rows_ref, tensor_ref, send_ref, block_ref):
    n_ia, n_ja, n_ka = sizes
    rows_i, rows_j, rows_k = tensor_ref.shape
    ja = place_ref[1]
    rows = rows_ref[...]
    sources = rows.shape[0]
    for t in range(2):
        one = rows[:, (t + 1) * R : (t + 2) * R]
        block_ref[pl.ds(t, sources, stride=2), :] = jnp.concatenate([one] * PACK, axis=1)
    tiled = block_ref[0:rows_k, :]
    lane = lax.broadcasted_iota(jnp.int32, (rows_k, LANES), 1) // R
    weights = jnp.concatenate(
        [jnp.where(lane == g, tiled, 0.0).astype(BF16) for g in range(PACK)], axis=0
    )
    group_i = rows_i // PACK
    sums = group_i // n_ka * rows_j
    left = jnp.concatenate(
        [
            tensor_ref[g * group_i : (g + 1) * group_i].reshape(group_i * rows_j, rows_k)
            for g in range(PACK)
        ],
        axis=1,
    )
    product = jnp.dot(left, weights, preferred_element_type=F32)
    send_ref[:, 0:sums, :] = product.astype(BF16).reshape(n_ka, sums, LANES)
    products = dot(rows, rows, ((0,), (0,)))
    gram_b = products[0:R, 0:R]
    gram_c = products[R : 2 * R, R : 2 * R] + products[2 * R : 3 * R, 2 * R : 3 * R]
    own_b = jnp.concatenate(
        [rows_ref[pl.ds(ia * n_ja + ja, 1), 0:R] for ia in range(n_ia)], axis=1
    )
    upper = lax.broadcasted_iota(jnp.int32, (R, R), 0) <= lax.broadcasted_iota(jnp.int32, (R, R), 1)
    diagonal = jnp.sum(gram_c * eye(), axis=0, keepdims=True)
    riders = jnp.concatenate(
        [
            pack(jnp.where(upper, gram_b, gram_c)),
            own_b,
            jnp.concatenate([diagonal, jnp.zeros((1, LANES - R), F32)], axis=1),
        ],
        axis=0,
    )
    high = riders.astype(BF16).astype(F32)
    middle = (riders - high).astype(BF16).astype(F32)
    low = riders - high - middle
    riders = jnp.concatenate([high, middle, low, jnp.zeros((2, LANES), F32)], axis=0).astype(BF16)
    for ka in range(n_ka):
        send_ref[ka, sums:, :] = riders


def first_kernel(low_i, got_ref, send_ref, along_ref, weights_ref, gram_ref, grams_ref):
    sums = got_ref.shape[1] - 4 * SUB
    n_ka = got_ref.shape[0]
    along = jnp.zeros((sums, LANES), F32)
    own_b = []
    total = jnp.zeros((SUB + 2, LANES), F32)
    for ka in range(n_ka):
        along += got_ref[ka, 0:sums, :].astype(F32)
        parts = got_ref[ka, sums:, :].astype(F32)
        size = SUB + 2
        riders = (parts[0:size] + parts[size : 2 * size]) + parts[2 * size : 3 * size]
        total += riders
        own_b.append(riders[SUB : SUB + 1])
    along_ref[...] = along
    grams_ref[...] = jnp.concatenate([total, jnp.zeros((SUB - 2, LANES), F32)], axis=0)
    own_b = jnp.concatenate(own_b, axis=0)
    block_b = unpack(own_b)
    rows_j = block_b.shape[0]
    wide_b = jnp.concatenate([block_b] * PACK, axis=1)
    terms = along.reshape(low_i, rows_j, LANES) * wide_b[None]
    summed = jnp.sum(terms, axis=1)
    rows = jnp.concatenate([summed] * (SUB // low_i), axis=0)
    for start in range(0, send_ref.shape[0], SUB):
        send_ref[start : start + SUB, :] = rows
    first_weights(grams_ref, weights_ref, gram_ref)


def first_weights(grams_ref, weights_ref, gram_ref):
    mixed = unpack(grams_ref[0:SUB])
    turned = mixed.T
    rows = lax.broadcasted_iota(jnp.int32, (R, R), 0)
    cols = lax.broadcasted_iota(jnp.int32, (R, R), 1)
    gram_b = jnp.where(rows <= cols, mixed, turned)
    gram_c = jnp.where(rows > cols, mixed, jnp.where(rows == cols, grams_ref[SUB + 1 : SUB + 2, 0:R], turned))
    gram_ref[...] = gram_c
    one = unpack(inverse(pack(gram_b * gram_c)))
    tiled = jnp.concatenate([jnp.concatenate([one] * PACK, axis=1)] * PACK, axis=0)
    rows = lax.broadcasted_iota(jnp.int32, (LANES, LANES), 0) // R
    cols = lax.broadcasted_iota(jnp.int32, (LANES, LANES), 1) // R
    weights_ref[...] = jnp.where(rows == cols, tiled, 0.0)


def second_kernel(low_i, got_ref, weights_ref, along_ref, send_ref):
    wide = jnp.sum(got_ref[...].reshape(got_ref.shape[0] // SUB, SUB, LANES), axis=0)
    summed = wide[0:low_i]
    for start in range(low_i, SUB, low_i):
        summed += wide[start : start + low_i]
    solved = dot(summed, weights_ref[...])
    rows_j = along_ref.shape[0] // low_i
    terms = along_ref[...].reshape(low_i, rows_j, LANES) * solved[:, None, :]
    wide = jnp.sum(terms, axis=0)
    part = wide[:, 0:R]
    for g in range(1, PACK):
        part += wide[:, g * R : (g + 1) * R]
    rows = jnp.concatenate([pack(part), solved] * 2, axis=0)
    for n in range(0, send_ref.shape[0], rows.shape[0]):
        send_ref[n : n + rows.shape[0], :] = rows


def third_kernel(
    totals, sizes, low_i, place_ref, got_ref, gram_c_ref, turned_ref,
    send_ref, gram_a_ref, factor_a_ref, solved_b_ref, everyone_ref,
):
    n_ia, n_ja, n_ka = sizes
    ia = place_ref[0]
    each = SUB + low_i
    pairs = got_ref.shape[0] // (2 * each)
    summed = jnp.sum(got_ref[...].reshape(pairs, 2 * each, LANES), axis=0)
    total = summed[0:SUB] + summed[each : each + SUB]
    lower = lax.broadcasted_iota(jnp.int32, (2 * low_i, LANES), 0) < low_i
    for n in range(pairs):
        start = 2 * each * n
        everyone_ref[2 * low_i * n : 2 * low_i * (n + 1), :] = jnp.where(
            lower,
            got_ref[start + SUB : start + 2 * SUB, :],
            got_ref[start + 2 * SUB : start + 3 * SUB, :],
        )
    everyone = everyone_ref[...]
    gram_raw = lane_groups(dot(everyone, everyone, ((0,), (0,))))
    row, column = scales(gram_raw, totals[0])
    gram_a = gram_raw * row * column
    gram_a_ref[...] = gram_a
    block = n_ka * low_i
    solved_a = unpack(everyone_ref[pl.ds(pl.multiple_of(ia * block, block), block), :])
    factor_a = solved_a * row
    factor_a_ref[...] = factor_a
    summed = (unpack(total) * row).T
    solved_b = dot(unpack(inverse(pack(gram_a * gram_c_ref[...]))), summed)
    solved_b_ref[...] = solved_b
    gram_b = pack(dot(solved_b, solved_b, ((1,), (1,))))
    a_low = factor_a.astype(BF16).T
    part = jnp.zeros((R, turned_ref.shape[2]), F32)
    rows_j, rows_k = turned_ref.shape[0], turned_ref.shape[2]
    step = 8
    for start in range(0, rows_j, step):
        right = jnp.concatenate([turned_ref[start + j] for j in range(step)], axis=1)
        along = jnp.dot(a_low, right, preferred_element_type=F32)
        for j in range(step):
            part += along[:, j * rows_k : (j + 1) * rows_k] * solved_b[:, start + j : start + j + 1]
    half = R // 2
    first = jnp.concatenate([part[:half], gram_b], axis=0)
    second = jnp.concatenate([part[half:], gram_b], axis=0)
    for n in range(n_ja // 2):
        send_ref[2 * n] = first
        send_ref[2 * n + 1] = second


def pass_kernel(got_ref, send_ref, gram_ref):
    total = jnp.sum(got_ref[...], axis=0)
    half = R // 2
    gram_ref[...] = total[half:]
    send_ref[...] = jnp.broadcast_to(total[None, :half], send_ref.shape)


def last_weights_kernel(totals, sizes, place_ref, gram_b_ref, gram_a_ref, factor_a_ref, solved_b_ref,
                        weights_ref, out_a_ref, out_b_ref):
    n_ia, n_ja, n_ka = sizes
    ia, ja, ka = place_ref[0], place_ref[1], place_ref[2]
    gram_raw = unpack(gram_b_ref[...])
    row, column = scales(gram_raw, totals[1])
    gram_b = gram_raw * row * column
    out_a_ref[...] = factor_a_ref[pl.ds(ja * n_ka + ka, 1), :]
    solved_b = solved_b_ref[...]
    j_of = lax.broadcasted_iota(jnp.int32, (8, solved_b.shape[1]), 1)
    chosen = jnp.where(j_of == ia * n_ka + ka, 1.0, 0.0)
    out_b_ref[...] = dot(chosen, solved_b, ((1,), (1,)))[0:1] * row
    weights_ref[...] = unpack(inverse(pack(gram_a_ref[...] * gram_b))) * column


def fourth_kernel(sizes, place_ref, got_ref, weights_ref, send_ref, own_c_ref, solved_ref):
    n_ia, n_ja, n_ka = sizes
    ia, ja = place_ref[0], place_ref[1]
    first = got_ref[0]
    second = got_ref[1]
    for n in range(1, n_ia):
        first += got_ref[2 * n]
        second += got_ref[2 * n + 1]
    solved = dot(jnp.concatenate([first, second], axis=0).T, weights_ref[...])
    solved_ref[...] = solved
    squares = jnp.sum(solved * solved, axis=0, keepdims=True)
    squares = jnp.concatenate([squares, jnp.zeros((1, LANES - R), F32)], axis=1)
    send_ref[...] = jnp.broadcast_to(squares, send_ref.shape)
    own = 2 * (ia * n_ja + ja)
    own_c_ref[...] = jnp.concatenate(
        [solved_ref[pl.ds(own, 1), :], solved_ref[pl.ds(own + 1, 1), :]], axis=0
    )


def last_kernel(total, got_ref, own_c_ref, out_ref):
    squares = jnp.sum(got_ref[...], axis=0, keepdims=True)[:, 0:R]
    out_ref[...] = own_c_ref[...] * lax.rsqrt(squares / total + 1e-06)


def exchange(blocks, axes, groups=None):
    return lax.all_to_all(blocks, axes, 0, 0, tiled=True, axis_index_groups=groups)


def exchange_rows(rows, axes):
    return exchange(rows[:, None, :], axes)[:, 0, :]


def local(tensor, factor_b, factor_c):
    rows_i, rows_j, rows_k = tensor.shape
    sizes = tuple(lax.axis_size(axis) for axis in ("ia", "ja", "ka"))
    n_ia, n_ja, n_ka = sizes
    totals = (rows_i * n_ia, rows_j * n_ja, rows_k * n_ka)
    cores = 2
    low_i = rows_i // (PACK * n_ka)
    place = jnp.stack([lax.axis_index(axis) for axis in ("ia", "ja", "ka")]).astype(jnp.int32)
    line = [
        [x * n_ja + z * cores + core for x in range(n_ia) for core in range(cores)]
        for z in range(n_ja // cores)
    ]
    (send,) = call(own_kernel, [shape(n_ia * n_ja, LANES)], [factor_b[0], factor_c[0]], 2**10)
    rows = exchange(send, ("ia", "ja"))
    turned = jnp.transpose(tensor, (1, 0, 2))
    rows, turned = lax.optimization_barrier((rows, turned))
    (send,) = call(
        lambda *refs: along_kernel(sizes, *refs),
        [shape(n_ka, low_i * rows_j + 4 * SUB, LANES, dtype=BF16)],
        [place, rows, tensor],
        2**26,
        scalars=1,
        scratch=[(rows_k + 8, LANES)],
    )
    got = exchange(send, "ka")
    send, along, weights_a, gram_c = call(
        lambda *refs: first_kernel(low_i, *refs),
        [shape(n_ja * low_i, LANES), shape(low_i * rows_j, LANES), shape(LANES, LANES), shape(R, R)],
        [got],
        2**20,
        scratch=[(2 * SUB, LANES)],
    )
    got = exchange_rows(send, "ja")
    (send,) = call(
        lambda *refs: second_kernel(low_i, *refs),
        [shape(n_ia * n_ka * (SUB + low_i), LANES)],
        [got, weights_a, along],
        2**20,
    )
    got = exchange_rows(send, ("ia", "ka"))
    send, gram_a, factor_a, solved_b = call(
        lambda *refs: third_kernel(totals, sizes, low_i, *refs),
        [
            shape(n_ja, R // 2 + SUB, LANES),
            shape(R, R),
            shape(rows_i, R),
            shape(R, rows_j),
        ],
        [place, got, gram_c, turned],
        2**26,
        scalars=1,
        scratch=[(n_ia * n_ka * low_i, LANES)],
    )
    got = exchange(send, "ja")
    send, gram_b = call(
        pass_kernel, [shape(n_ia * cores, R // 2, LANES), shape(SUB, LANES)], [got], 2**16
    )
    got = exchange(send, ("ia", "ja"), line)
    weights_c, out_a, out_b = call(
        lambda *refs: last_weights_kernel(totals, sizes, *refs),
        [shape(R, R), shape(1, R), shape(1, R)],
        [place, gram_b, gram_a, factor_a, solved_b],
        2**24,
        scalars=1,
    )
    send, own_c = call(
        lambda *refs: fourth_kernel(sizes, *refs),
        [shape(n_ka, LANES), shape(2, R)],
        [place, got, weights_c],
        2**20,
        scalars=1,
        scratch=[(rows_k, R)],
    )
    got = exchange_rows(send, "ka")
    (out_c,) = call(
        lambda *refs: last_kernel(totals[2], *refs), [shape(2, R)], [got, own_c], 2**12
    )
    return out_a[None], out_b[None], out_c[None]


def solution(mesh):
    placed = (P("ia", "ja", "ka"), P("ja", ("ia", "ka"), None), P("ka", ("ia", "ja"), None))
    return jax.shard_map(
        local,
        mesh=mesh,
        in_specs=placed,
        out_specs=(
            P("ia", ("ja", "ka"), None),
            P("ja", ("ia", "ka"), None),
            P("ka", ("ia", "ja"), None),
        ),
        check_vma=False,
    )
```
